32 devices in a mesh: panel: 4 (over y, core), blk: 8 (over z, x).
Axes of the slice: x: 2, y: 2, z: 4, core: 2. Of those that a mesh axis runs over, the one named last changes fastest.
Arguments:
- source_flux: bfloat16 [72, 256, 1024], P(None, 'panel', 'blk'), may hold values from -6 to 6
- gauss_weight: float32 [4, 256, 512], P(None, ('panel', 'blk')), may hold values from 0.02 to 0.2
- gauss_offset: float32 [2, 4, 256, 512], P(None, None, ('panel', 'blk')), may hold values from -0.5 to 0.5
- slot_count: int32 [256], P(('panel', 'blk')), may hold values from 1 to 512, as said below
- source_cell: int32 [256, 512], P(('panel', 'blk')), may hold values from 0 to 8191, as said below
- target_cell: int32 [256, 512], P(('panel', 'blk')), may hold values from 0 to 4095, as said below
- target_area: float32 [131072], P(('panel', 'blk')), may hold values from 0.25 to 1
Outputs:
- remapped: bfloat16 [72, 131072], P(None, ('panel', 'blk'))
The draws below stay inside these ranges and needn't reach their ends.
Inputs may be any that keep to these rules, and one draw needn't show every extreme that they name: `slot_count`: live slots from source s to owner k of its band at entry s * size of blk + k; in every draw some owner receives 512 live slots from every source device of its band. `source_cell`: Row-major index of a cell in the sender's block of 64 x 128; slots past the count hold arbitrary cells. `target_cell`: cell index within owner d's 4096 cells; row d * size of blk + k lists the slots from source k of d's band.
All inputs are finite; a program needn't handle non-finite values.
Results may differ from the reference program's by a relative error of at most 0.0044.
The reference program's roundings to bfloat16 on the way count: a program that leaves them out, or rounds other values in their place, can miss the bound.
Values may be sent and summed in bfloat16 or wider, within the bound.
A program may use at most 192 MiB of HBM per device.

```python
import math
import jax
import jax.numpy as jnp
from jax import lax

F = 72
Q = 4
SX = 64
SY = 128
OWNERS = 32
CAP = 512
TC = 4096
NSX = 256
NSY = 1024
N_PANEL = 4
N_BLK = 8


def draw_slot_count(key, part):
    key_load, key_heavy, key_drop = jax.random.split(jax.random.fold_in(key, 7), 3)
    load = jax.random.randint(key_load, (OWNERS,), CAP // 8 + 1, CAP + 1)
    heavy = jax.random.randint(key_heavy, (), 0, OWNERS)
    is_heavy = jnp.arange(OWNERS) == heavy
    load = jnp.where(is_heavy, CAP, load)
    sources = jnp.arange(OWNERS)[:, None]
    members = jnp.arange(N_BLK)[None, :]
    owner_id = sources // N_BLK * N_BLK + members
    drop = jax.random.randint(key_drop, (OWNERS, N_BLK), 0, CAP // 4 + 1)
    counts = jnp.maximum(load[owner_id] - drop, 1)
    counts = jnp.where(is_heavy[owner_id], CAP, counts)
    return counts.reshape(OWNERS * N_BLK).astype(jnp.int32)


def draw_source_cell(key, part):
    key_row, key_col = jax.random.split(jax.random.fold_in(key, 11), 2)
    rows = jnp.arange(OWNERS * N_BLK)[:, None]
    sender = rows // N_BLK
    member = rows % N_BLK
    offset = (member - sender % N_BLK) % N_BLK
    cell_row = jax.random.randint(key_row, (OWNERS * N_BLK, CAP), 0, SX)
    spread = jax.random.randint(key_col, (OWNERS * N_BLK, CAP), 0, max(SY // 2, 1))
    cell_col = (offset * SY // N_BLK + spread) % SY
    return (cell_row * SY + cell_col).astype(jnp.int32)


def draw_target_cell(key, part):
    key_spot = jax.random.fold_in(key, 13)
    rows = jnp.arange(OWNERS * N_BLK)[:, None]
    owner = rows // N_BLK
    member = rows % N_BLK
    offset = (member - owner % N_BLK) % N_BLK
    spread = jax.random.randint(key_spot, (OWNERS * N_BLK, CAP), 0, max(TC // 2, 1))
    return ((offset * TC // N_BLK + spread) % TC).astype(jnp.int32)


def steps_of(stream_key, extent, cuts, smallest, high):
    def one(dim, parts):
        draws = jax.random.uniform(jax.random.fold_in(jax.random.fold_in(stream_key, 6), dim), (parts,), jnp.float32, smallest / len(cuts), high / len(cuts))
        return jnp.repeat(jnp.exp(draws), extent[dim] // parts).reshape((-1,) + (1,) * (len(extent) - dim - 1))

    factor_of = one(*cuts[0])
    for cut in cuts[1:]:
        factor_of = factor_of * one(*cut)
    return factor_of


def gaussian(key, extent, deviation, reach, shards=(), kind=jnp.bfloat16):
    values = deviation * jax.random.normal(key, extent, jnp.float32)
    if shards:
        values = values * steps_of(key, extent, shards, -0.22, 0.18)
    return jnp.clip(values, -reach, reach).astype(kind)


def setup_inputs(seed: int = 0) -> dict:
    splits = jax.random.split(jax.random.key(seed), 8)
    source_flux = gaussian(splits[0], (F, NSX, NSY), 1.0, 6.0, ((1, 4), (2, 8)))
    gauss_weight = jnp.clip(jnp.exp(math.log(0.2) - 2.3025851 * jax.random.uniform(splits[1], (Q, OWNERS * N_BLK, CAP), jnp.float32) ** steps_of(splits[1], (Q, OWNERS * N_BLK, CAP), ((1, 32),), -0.2, 0.2)), 0.02, 0.2)
    gauss_offset = jnp.clip(jax.random.uniform(splits[2], (2, Q, OWNERS * N_BLK, CAP), jnp.float32, -0.5, 0.5) * steps_of(splits[2], (2, Q, OWNERS * N_BLK, CAP), ((2, 32),), -0.4, 0.0), -0.5, 0.5)
    slot_count = draw_slot_count(jax.random.fold_in(splits[7], 71), 0)
    source_cell = draw_source_cell(jax.random.fold_in(splits[7], 71), 0)
    target_cell = draw_target_cell(jax.random.fold_in(splits[7], 71), 0)
    target_area = jnp.clip(jnp.exp(math.log(1.0) - 1.3862944 * jax.random.uniform(splits[6], (OWNERS * TC,), jnp.float32) ** steps_of(splits[6], (OWNERS * TC,), ((0, 32),), -0.2, 0.2)), 0.25, 1.0)
    return {"source_flux": source_flux, "gauss_weight": gauss_weight, "gauss_offset": gauss_offset, "slot_count": slot_count, "source_cell": source_cell, "target_cell": target_cell, "target_area": target_area}


def rim_slice(block, along, offset, height, breadth):
    if along == 0:
        return block[:, 2 + offset:2 + offset + height, 2:2 + breadth]
    return block[:, 2:2 + height, 2 + offset:2 + offset + breadth]


def reconstruct(block, height, breadth):
    center = rim_slice(block, 0, 0, height, breadth)
    along_x = [rim_slice(block, 0, offset, height, breadth) for offset in (-2, -1, 1, 2)]
    along_y = [rim_slice(block, 1, offset, height, breadth) for offset in (-2, -1, 1, 2)]
    slope_x = (along_x[0] - 8.0 * along_x[1] + 8.0 * along_x[2] - along_x[3]) / 12.0
    curve_x = (-along_x[0] + 16.0 * along_x[1] - 30.0 * center + 16.0 * along_x[2] - along_x[3]) / 12.0
    slope_y = (along_y[0] - 8.0 * along_y[1] + 8.0 * along_y[2] - along_y[3]) / 12.0
    curve_y = (-along_y[0] + 16.0 * along_y[1] - 30.0 * center + 16.0 * along_y[2] - along_y[3]) / 12.0
    stacked = jnp.stack([center, slope_x, slope_y, curve_x, curve_y])
    return stacked.reshape(5, block.shape[0], height * breadth)


def reference(source_flux, gauss_weight, gauss_offset, slot_count, source_cell, target_cell, target_area):
    owners = N_PANEL * N_BLK
    wrapped = jnp.concatenate([source_flux[:, :, -2:], source_flux, source_flux[:, :, :2]], axis=2)
    padded = jnp.pad(wrapped, ((0, 0), (2, 2), (0, 0)))
    weight = gauss_weight.reshape(Q, owners, N_BLK, CAP)
    offset_x = gauss_offset[0].reshape(Q, owners, N_BLK, CAP)
    offset_y = gauss_offset[1].reshape(Q, owners, N_BLK, CAP)
    moments = jnp.stack([
        jnp.sum(weight, axis=0),
        jnp.sum(weight * offset_x, axis=0),
        jnp.sum(weight * offset_y, axis=0),
        0.5 * jnp.sum(weight * offset_x * offset_x, axis=0),
        0.5 * jnp.sum(weight * offset_y * offset_y, axis=0)])
    slots = jnp.arange(CAP).astype(jnp.int32)
    live_mask = (slots[None, None, :] < slot_count.reshape(owners, N_BLK)[:, :, None]).astype(jnp.float32)
    coefficient = moments * live_mask[None]
    cells = source_cell.reshape(owners, N_BLK, CAP)
    targets = target_cell.reshape(owners, N_BLK, CAP)
    band_rows = jnp.arange(N_BLK).astype(jnp.int32)

    def accumulate(summed, source):
        source = source.astype(jnp.int32)
        band = (source // N_BLK).astype(jnp.int32)
        column = (source % N_BLK).astype(jnp.int32)
        row_start = (band * SX).astype(jnp.int32)
        col_start = (column * SY).astype(jnp.int32)
        block = lax.dynamic_slice(padded, (jnp.int32(0), row_start, col_start), (F, SX + 4, SY + 4)).astype(jnp.float32)
        recon = reconstruct(block, SX, SY)
        picked = jnp.take(recon, cells[source].reshape(-1), axis=2).reshape(5, F, N_BLK, CAP)
        record_value = jnp.sum(picked * coefficient[:, source][:, None], axis=0)
        rounded = lax.optimization_barrier(record_value.astype(jnp.bfloat16)).astype(jnp.float32)
        dest_owner = (band * N_BLK + band_rows).astype(jnp.int32)
        dest_cells = targets[dest_owner, column, :]
        summed = summed.at[dest_owner[:, None], dest_cells].add(jnp.transpose(rounded, (1, 2, 0)))
        return summed, None

    start = jnp.zeros((owners, TC, F), jnp.float32)
    summed, unused = lax.scan(accumulate, start, jnp.arange(owners).astype(jnp.int32))
    result = summed / target_area.reshape(owners, TC)[:, :, None]
    return jnp.transpose(result, (2, 0, 1)).reshape(F, owners * TC).astype(jnp.bfloat16)
```

```python
import jax
import jax.numpy as jnp
import numpy as np
from jax import lax
from jax.experimental import pallas as pl
from jax.experimental.pallas import tpu as pltpu
from jax.sharding import PartitionSpec as P

LANES = 128
GROUP = 16
TAPS = 16
LEFT = 8
LOW = 256


def tap_pattern():
    first = np.array([1, -8, 0, 8, -1, 0, 0, 0]) / 12.0
    second = np.array([-1, 16, -30, 16, -1, 0, 0, 0]) / 12.0
    here = np.array([0, 0, 1, 0, 0, 0, 0, 0])
    none = np.zeros(8)
    rows = [
        np.concatenate([here, none]),
        np.concatenate([none, first]),
        np.concatenate([first, none]),
        np.concatenate([none, second]),
        np.concatenate([second, none]),
    ]
    rows += [np.zeros(TAPS)] * 3
    return np.tile(np.stack(rows), (1, GROUP)).astype(np.float32)


def gather_kernel(
    count, cells, flux, above, below, before, after, weight, offset, pattern, out, wide, grid, mom
):
    fields, height, breadth = flux.shape
    members, capacity = cells.shape
    pitch = breadth + 2 * LEFT
    chunks = capacity // LANES
    fill = jnp.zeros((LANES - fields, breadth), jnp.float32)

    grid[...] = jnp.zeros_like(grid)

    def widen(f, carry):
        wide[pl.ds(f * height, height), :] = flux[f].astype(jnp.float32)
        return carry

    lax.fori_loop(0, fields, widen, 0, unroll=8)

    def place(row, block):
        turned = jnp.concatenate([block, fill], axis=0).T
        grid[pl.ds(pl.multiple_of(row * pitch + LEFT, 8), breadth), :] = turned

    for r in range(2):
        place(r, above[r].astype(jnp.float32))
        place(height + 2 + r, below[r].astype(jnp.float32))

    def turn(i, carry):
        place(i + 2, wide[pl.ds(i, fields, stride=height), :])
        return carry

    lax.fori_loop(0, height, turn, 0, unroll=4)
    for q in range(2):
        grid[pl.ds(2 * pitch + LEFT - 2 + q, height, stride=pitch), :] = before[q].astype(jnp.float32)
        grid[pl.ds(2 * pitch + LEFT + breadth + q, height, stride=pitch), :] = after[q].astype(
            jnp.float32
        )

    w = weight[...]
    ox = offset[0]
    oy = offset[1]
    moments = [
        jnp.sum(w, axis=0),
        jnp.sum(w * ox, axis=0),
        jnp.sum(w * oy, axis=0),
        0.5 * jnp.sum(w * ox * ox, axis=0),
        0.5 * jnp.sum(w * oy * oy, axis=0),
    ]
    mom[...] = jnp.zeros_like(mom)
    for m, moment in enumerate(moments):
        for k in range(members):
            mom[k, m : m + 1, :] = moment[k : k + 1, :]

    slot_group = lax.broadcasted_iota(jnp.int32, (LANES, GROUP * TAPS), 0) % GROUP
    tap_group = lax.broadcasted_iota(jnp.int32, (LANES, GROUP * TAPS), 1) // TAPS
    diagonal = slot_group == tap_group

    def chunk(step, carry):
        k = step // chunks
        q = step % chunks
        start = pl.multiple_of(q * LANES, LANES)
        live = count[k] - start

        @pl.when(live > 0)
        def _():
            lane = lax.broadcasted_iota(jnp.int32, (8, LANES), 1)
            m = jnp.where(lane < live, mom[k, :, pl.ds(start, LANES)], 0.0)
            coef = jnp.dot(
                m.T,
                pattern[...],
                precision=lax.Precision.HIGHEST,
                preferred_element_type=jnp.float32,
            )
            coef = jnp.where(diagonal, coef, 0.0)
            high = coef.astype(jnp.bfloat16)
            low = (coef - high.astype(jnp.float32)).astype(jnp.bfloat16)
            parts = []
            for g in range(LANES // GROUP):
                taps = []
                for s in range(GROUP):
                    cell = cells[k, start + g * GROUP + s]
                    base = cell + (cell // breadth) * (pitch - breadth)
                    taps.append(grid[pl.ds(base + 2 * pitch + LEFT - 2, 8), :])
                    taps.append(grid[pl.ds(base + LEFT, 8, stride=pitch), :])
                picked = jnp.concatenate(taps, axis=0).astype(jnp.bfloat16)
                rows = slice(g * GROUP, (g + 1) * GROUP)
                both = jnp.concatenate([high[rows], low[rows]], axis=0)
                r = jnp.dot(both, picked, preferred_element_type=jnp.float32)
                parts.append(r[:GROUP] + r[GROUP:])
            record = jnp.concatenate(parts, axis=0).T
            out[k, :, pl.ds(start, LANES)] = record[:fields].astype(jnp.bfloat16)

        @pl.when(live <= 0)
        def _():
            out[k, :, pl.ds(start, LANES)] = jnp.zeros((fields, LANES), jnp.bfloat16)

        return carry

    lax.fori_loop(0, members * chunks, chunk, 0)


def scatter_kernel(records, target, area, out, masked, total):
    members, fields, capacity = records.shape
    digits = out.shape[1] // LOW
    rows = total.shape[0] // digits
    fill = jnp.zeros((rows - fields, capacity), jnp.bfloat16)
    total[...] = jnp.zeros_like(total)

    def member(k, carry):
        cell = target[pl.ds(k, 1), :]
        high = cell // LOW
        low = cell % LOW
        spots = lax.broadcasted_iota(jnp.int32, (LOW, capacity), 0)
        table = jnp.where(spots == low, 1.0, 0.0).astype(jnp.bfloat16)
        record = jnp.concatenate([records[k], fill], axis=0)
        for h in range(digits):
            here = jnp.where(high == h, 1.0, 0.0).astype(jnp.bfloat16)
            masked[h * rows : (h + 1) * rows, :] = record * here
        total[...] += lax.dot_general(
            masked[...], table, (((1,), (1,)), ((), ())), preferred_element_type=jnp.float32
        )
        return carry

    lax.fori_loop(0, members, member, 0)
    for h in range(digits):
        columns = slice(h * LOW, (h + 1) * LOW)
        value = total[h * rows : h * rows + fields, :] / area[:, columns]
        out[:, columns] = value.astype(jnp.bfloat16)


def on_device(
    source_flux, gauss_weight, gauss_offset, slot_count, source_cell, target_cell, target_area
):
    fields, height, breadth = source_flux.shape
    members, capacity = source_cell.shape
    ocean_cells = target_area.shape[0]
    pitch = breadth + 2 * LEFT

    panels = lax.axis_size("panel")
    columns = lax.axis_size("blk")
    up = [(i, i + 1) for i in range(panels - 1)]
    down = [(i + 1, i) for i in range(panels - 1)]
    east = [(i, (i + 1) % columns) for i in range(columns)]
    west = [(j, i) for i, j in east]
    first_rows = jnp.transpose(source_flux[:, :2, :], (1, 0, 2))
    last_rows = jnp.transpose(source_flux[:, height - 2 :, :], (1, 0, 2))
    first_cols = jnp.transpose(source_flux[:, :, :2], (2, 1, 0))
    last_cols = jnp.transpose(source_flux[:, :, breadth - 2 :], (2, 1, 0))
    wide_lanes = ((0, 0), (0, 0), (0, LANES - fields))
    above = lax.ppermute(last_rows, "panel", up)
    below = lax.ppermute(first_rows, "panel", down)
    before = lax.ppermute(jnp.pad(last_cols, wide_lanes), "blk", east)
    after = lax.ppermute(jnp.pad(first_cols, wide_lanes), "blk", west)

    vmem = pl.BlockSpec(memory_space=pltpu.VMEM)
    smem = pl.BlockSpec(memory_space=pltpu.SMEM)
    records = pl.pallas_call(
        gather_kernel,
        out_shape=jax.ShapeDtypeStruct((members, fields, capacity), jnp.bfloat16),
        in_specs=[smem, smem] + [vmem] * 8,
        out_specs=vmem,
        scratch_shapes=[
            pltpu.VMEM((fields * height, breadth), jnp.float32),
            pltpu.VMEM(((height + 8) * pitch, LANES), jnp.float32),
            pltpu.VMEM((members, 8, capacity), jnp.float32),
        ],
        compiler_params=pltpu.CompilerParams(vmem_limit_bytes=48 * 2**20),
        name="gather_records",
    )(
        slot_count,
        source_cell,
        source_flux,
        above,
        below,
        before,
        after,
        gauss_weight,
        gauss_offset,
        jnp.asarray(tap_pattern()),
    )
    arrived = lax.all_to_all(records, "blk", split_axis=0, concat_axis=0, tiled=True)
    digits = ocean_cells // LOW
    rows = -(-fields // 16) * 16
    return pl.pallas_call(
        scatter_kernel,
        out_shape=jax.ShapeDtypeStruct((fields, ocean_cells), jnp.bfloat16),
        in_specs=[vmem] * 3,
        out_specs=vmem,
        scratch_shapes=[
            pltpu.VMEM((digits * rows, capacity), jnp.bfloat16),
            pltpu.VMEM((digits * rows, LOW), jnp.float32),
        ],
        compiler_params=pltpu.CompilerParams(vmem_limit_bytes=48 * 2**20),
        name="scatter_records",
    )(arrived, target_cell, target_area.reshape(1, ocean_cells))


def solution(mesh):
    placed = (
        P(None, "panel", "blk"),
        P(None, ("panel", "blk"), None),
        P(None, None, ("panel", "blk"), None),
        P(("panel", "blk")),
        P(("panel", "blk"), None),
        P(("panel", "blk"), None),
        P(("panel", "blk")),
    )
    return jax.shard_map(
        on_device, mesh=mesh, in_specs=placed, out_specs=P(None, ("panel", "blk")), check_vma=False
    )
```

```python
import jax
import jax.numpy as jnp
import numpy as np
from jax import lax
from jax.experimental import pallas as pl
from jax.experimental.pallas import tpu as pltpu
from jax.sharding import PartitionSpec as P

LANES = 128
GROUP = 16
TAPS = 16
LEFT = 8
PARTS = 3
LOW = 256


def tap_pattern():
    first = np.array([1, -8, 0, 8, -1, 0, 0, 0])
    second = np.array([-1, 16, -30, 16, -1, 0, 0, 0])
    here = np.array([0, 0, 1, 0, 0, 0, 0, 0])
    none = np.zeros(8)
    rows = [
        np.concatenate([here, none]),
        np.concatenate([none, first]),
        np.concatenate([first, none]),
        np.concatenate([none, second]),
        np.concatenate([second, none]),
    ]
    rows += [np.zeros(TAPS)] * 3
    return np.tile(np.stack(rows), (PARTS, GROUP)).astype(np.float32)


def gather_kernel(
    count, cells, flux, above, below, before, after, weight, offset, pattern, out, wide, grid, mom
):
    fields, height, breadth = flux.shape
    members, capacity = cells.shape
    pitch = breadth + 2 * LEFT
    chunks = capacity // LANES
    shift = breadth.bit_length() - 1
    assert breadth == 1 << shift
    fill = jnp.zeros((LANES - fields, breadth), jnp.float32)

    grid[...] = jnp.zeros_like(grid)

    def widen(f, carry):
        wide[pl.ds(f * height, height), :] = flux[f].astype(jnp.float32)
        return carry

    lax.fori_loop(0, fields, widen, 0, unroll=8)

    def place(row, block):
        turned = jnp.concatenate([block, fill], axis=0).T
        grid[pl.ds(pl.multiple_of(row * pitch + LEFT, 8), breadth), :] = turned

    for r in range(2):
        place(r, above[r].astype(jnp.float32))
        place(height + 2 + r, below[r].astype(jnp.float32))

    def turn(i, carry):
        place(i + 2, wide[pl.ds(i, fields, stride=height), :])
        return carry

    lax.fori_loop(0, height, turn, 0, unroll=4)
    for q in range(2):
        grid[pl.ds(2 * pitch + LEFT - 2 + q, height, stride=pitch), :] = before[q].astype(jnp.float32)
        grid[pl.ds(2 * pitch + LEFT + breadth + q, height, stride=pitch), :] = after[q].astype(
            jnp.float32
        )

    w = weight[...]
    ox = offset[0]
    oy = offset[1]
    moments = [
        jnp.sum(w, axis=0),
        jnp.sum(w * ox, axis=0) / 12.0,
        jnp.sum(w * oy, axis=0) / 12.0,
        0.5 * jnp.sum(w * ox * ox, axis=0) / 12.0,
        0.5 * jnp.sum(w * oy * oy, axis=0) / 12.0,
    ]
    mom[...] = jnp.zeros_like(mom)
    slots = lax.broadcasted_iota(jnp.int32, (1, capacity), 1)
    alive = [slots < count[k] for k in range(members)]
    for m, moment in enumerate(moments):
        for part in range(PARTS):
            piece = moment.astype(jnp.bfloat16).astype(jnp.float32)
            moment = moment - piece
            for k in range(members):
                mom[k, part * 8 + m : part * 8 + m + 1, :] = jnp.where(alive[k], piece[k : k + 1, :], 0.0)

    slot_group = lax.broadcasted_iota(jnp.int32, (LANES, GROUP * TAPS), 0) % GROUP
    tap_group = lax.broadcasted_iota(jnp.int32, (LANES, GROUP * TAPS), 1) // TAPS
    diagonal = slot_group == tap_group

    def chunk(step, carry):
        k = step // chunks
        q = step % chunks
        start = pl.multiple_of(q * LANES, LANES)
        live = count[k] - start

        @pl.when(live > 0)
        def _():
            m = mom[k, :, pl.ds(start, LANES)].T.astype(jnp.bfloat16)
            coef = jnp.dot(m, pattern[...], preferred_element_type=jnp.float32)
            coef = jnp.where(diagonal, coef, 0.0)
            high = coef.astype(jnp.bfloat16)
            low = (coef - high.astype(jnp.float32)).astype(jnp.bfloat16)
            parts = []
            for g in range(LANES // GROUP):
                taps = []
                for s in range(GROUP):
                    cell = cells[k, start + g * GROUP + s]
                    base = cell + lax.shift_right_logical(cell, shift) * (pitch - breadth)
                    taps.append(grid[pl.ds(base + 2 * pitch + LEFT - 2, 8), :])
                    taps.append(grid[pl.ds(base + LEFT, 8, stride=pitch), :])
                picked = jnp.concatenate(taps, axis=0).astype(jnp.bfloat16)
                rows = slice(g * GROUP, (g + 1) * GROUP)
                both = jnp.concatenate([high[rows], low[rows]], axis=0)
                r = jnp.dot(both, picked, preferred_element_type=jnp.float32)
                parts.append(r[:GROUP] + r[GROUP:])
            record = jnp.concatenate(parts, axis=0).T
            out[k, :, pl.ds(start, LANES)] = record[:fields].astype(jnp.bfloat16)

        @pl.when(live <= 0)
        def _():
            out[k, :, pl.ds(start, LANES)] = jnp.zeros((fields, LANES), jnp.bfloat16)

        return carry

    lax.fori_loop(0, members * chunks, chunk, 0)


def scatter_kernel(records, target, area, out, landed, masked, total, sent, came):
    members, fields, capacity = records.shape
    digits = out.shape[1] // LOW
    rows = total.shape[0] // digits
    fill = jnp.zeros((rows - fields, capacity), jnp.bfloat16)
    me = lax.axis_index("blk")

    def peer(step):
        return {"blk": lax.rem(me + step, members)}

    def copy(step):
        return pltpu.make_async_remote_copy(
            src_ref=records.at[lax.rem(me + step, members)],
            dst_ref=landed.at[step - 1],
            send_sem=sent.at[step - 1],
            recv_sem=came.at[step - 1],
            device_id=peer(step),
            device_id_type=pl.DeviceIdType.MESH,
        )

    barrier = pltpu.get_barrier_semaphore()
    for step in range(1, members):
        pl.semaphore_signal(barrier, 1, device_id=peer(step), device_id_type=pl.DeviceIdType.MESH)
    pl.semaphore_wait(barrier, members - 1)
    for step in range(1, members):
        copy(step).start()

    def deposit(record, source):
        cell = target[pl.ds(source, 1), :]
        high = lax.shift_right_logical(cell, LOW.bit_length() - 1)
        low = cell & (LOW - 1)
        spots = lax.broadcasted_iota(jnp.int32, (LOW, capacity), 0)
        table = jnp.where(spots == low, 1.0, 0.0).astype(jnp.bfloat16)
        record = jnp.concatenate([record, fill], axis=0)
        for h in range(digits):
            here = jnp.where(high == h, 1.0, 0.0).astype(jnp.bfloat16)
            masked[h * rows : (h + 1) * rows, :] = record * here
        return lax.dot_general(
            masked[...], table, (((1,), (1,)), ((), ())), preferred_element_type=jnp.float32
        )

    total[...] = deposit(records[me], me)

    def arrival(step, carry):
        copy(step).wait_recv()
        total[...] += deposit(landed[step - 1], lax.rem(me - step + members, members))
        return carry

    lax.fori_loop(1, members, arrival, 0)
    for h in range(digits):
        columns = slice(h * LOW, (h + 1) * LOW)
        value = total[h * rows : h * rows + fields, :] / area[:, columns]
        out[:, columns] = value.astype(jnp.bfloat16)
    for step in range(1, members):
        copy(step).wait_send()


def on_device(
    source_flux, gauss_weight, gauss_offset, slot_count, source_cell, target_cell, target_area
):
    fields, height, breadth = source_flux.shape
    members, capacity = source_cell.shape
    ocean_cells = target_area.shape[0]
    pitch = breadth + 2 * LEFT

    panels = lax.axis_size("panel")
    columns = lax.axis_size("blk")
    up = [(i, i + 1) for i in range(panels - 1)]
    down = [(i + 1, i) for i in range(panels - 1)]
    east = [(i, (i + 1) % columns) for i in range(columns)]
    west = [(j, i) for i, j in east]
    first_rows = jnp.transpose(source_flux[:, :2, :], (1, 0, 2))
    last_rows = jnp.transpose(source_flux[:, height - 2 :, :], (1, 0, 2))
    first_cols = jnp.transpose(source_flux[:, :, :2], (2, 1, 0))
    last_cols = jnp.transpose(source_flux[:, :, breadth - 2 :], (2, 1, 0))
    wide_lanes = ((0, 0), (0, 0), (0, LANES - fields))
    above = lax.ppermute(last_rows, "panel", up)
    below = lax.ppermute(first_rows, "panel", down)
    before = lax.ppermute(jnp.pad(last_cols, wide_lanes), "blk", east)
    after = lax.ppermute(jnp.pad(first_cols, wide_lanes), "blk", west)

    vmem = pl.BlockSpec(memory_space=pltpu.VMEM)
    smem = pl.BlockSpec(memory_space=pltpu.SMEM)
    records = pl.pallas_call(
        gather_kernel,
        out_shape=jax.ShapeDtypeStruct((members, fields, capacity), jnp.bfloat16),
        in_specs=[smem, smem] + [vmem] * 8,
        out_specs=vmem,
        scratch_shapes=[
            pltpu.VMEM((fields * height, breadth), jnp.float32),
            pltpu.VMEM(((height + 8) * pitch, LANES), jnp.float32),
            pltpu.VMEM((members, 8 * PARTS, capacity), jnp.float32),
        ],
        compiler_params=pltpu.CompilerParams(vmem_limit_bytes=48 * 2**20),
        name="gather_records",
    )(
        slot_count,
        source_cell,
        source_flux,
        above,
        below,
        before,
        after,
        gauss_weight,
        gauss_offset,
        jnp.asarray(tap_pattern(), jnp.bfloat16),
    )
    digits = ocean_cells // LOW
    rows = -(-fields // 16) * 16
    return pl.pallas_call(
        scatter_kernel,
        out_shape=jax.ShapeDtypeStruct((fields, ocean_cells), jnp.bfloat16),
        in_specs=[vmem] * 3,
        out_specs=vmem,
        scratch_shapes=[
            pltpu.VMEM((members - 1, fields, capacity), jnp.bfloat16),
            pltpu.VMEM((digits * rows, capacity), jnp.bfloat16),
            pltpu.VMEM((digits * rows, LOW), jnp.float32),
            pltpu.SemaphoreType.DMA((members - 1,)),
            pltpu.SemaphoreType.DMA((members - 1,)),
        ],
        compiler_params=pltpu.CompilerParams(
            vmem_limit_bytes=48 * 2**20, collective_id=0, has_side_effects=True
        ),
        name="scatter_records",
    )(records, target_cell, target_area.reshape(1, ocean_cells))


def solution(mesh):
    placed = (
        P(None, "panel", "blk"),
        P(None, ("panel", "blk"), None),
        P(None, None, ("panel", "blk"), None),
        P(("panel", "blk")),
        P(("panel", "blk"), None),
        P(("panel", "blk"), None),
        P(("panel", "blk")),
    )
    return jax.shard_map(
        on_device, mesh=mesh, in_specs=placed, out_specs=P(None, ("panel", "blk")), check_vma=False
    )
```

```python
import jax
import jax.numpy as jnp
import numpy as np
from jax import lax
from jax.experimental import pallas as pl
from jax.experimental.pallas import tpu as pltpu
from jax.sharding import PartitionSpec as P

LANES = 128
GROUP = 16
TAPS = 16
LEFT = 8
PARTS = 3
LOW = 256


def tap_pattern():
    first = np.array([1, -8, 0, 8, -1, 0, 0, 0])
    second = np.array([-1, 16, -30, 16, -1, 0, 0, 0])
    here = np.array([0, 0, 1, 0, 0, 0, 0, 0])
    none = np.zeros(8)
    rows = [
        np.concatenate([here, none]),
        np.concatenate([none, first]),
        np.concatenate([first, none]),
        np.concatenate([none, second]),
        np.concatenate([second, none]),
    ]
    rows += [np.zeros(TAPS)] * 3
    return np.tile(np.stack(rows), (PARTS, GROUP)).astype(np.float32)


def halo_kernel(
    flux, above, below, before, after, wide, edges, row_out, col_out, row_in, col_in, sent, came
):
    fields, height, breadth = flux.shape
    axes = ("panel", "panel", "blk", "blk")
    shifts = (1, -1, 1, -1)

    def neighbour(n):
        size = lax.axis_size(axes[n])
        return {axes[n]: lax.rem(lax.axis_index(axes[n]) + shifts[n] + size, size)}

    barrier = pltpu.get_barrier_semaphore()
    for n in range(4):
        pl.semaphore_signal(
            barrier, 1, device_id=neighbour(n), device_id_type=pl.DeviceIdType.MESH
        )

    def widen(f, carry):
        wide[pl.ds(f * height, height), :] = flux[f].astype(jnp.float32)
        return carry

    lax.fori_loop(0, fields, widen, 0, unroll=8)
    for side, first in enumerate((height - 2, 0)):
        for r in range(2):
            row = wide[pl.ds(first + r, fields, stride=height), :]
            row_out[side, r] = row.astype(jnp.bfloat16)

    line = lax.broadcasted_iota(jnp.int32, (16, breadth), 0)
    column = lax.broadcasted_iota(jnp.int32, (16, breadth), 1)
    wanted = jnp.where(line < 2, breadth - 2 + line, line - 2)
    chosen = jnp.where((column == wanted) & (line < 4), 1.0, 0.0).astype(jnp.bfloat16)
    fill = jnp.zeros((LANES - fields, breadth), jnp.float32)

    def pick(i, carry):
        block = jnp.concatenate([wide[pl.ds(i, fields, stride=height), :], fill], axis=0)
        picked = lax.dot_general(
            chosen,
            block.astype(jnp.bfloat16),
            (((1,), (1,)), ((), ())),
            preferred_element_type=jnp.float32,
        )
        edges[pl.ds(pl.multiple_of(i * 8, 8), 8), :] = picked[:8]
        return carry

    lax.fori_loop(0, height, pick, 0, unroll=8)
    for side in range(2):
        for q in range(2):
            col = edges[pl.ds(2 * side + q, height, stride=8), :]
            col_out[side, q] = col.astype(jnp.bfloat16)

    pl.semaphore_wait(barrier, 4)
    copies = []
    for n in range(4):
        source, target = (row_out, row_in) if n < 2 else (col_out, col_in)
        copies.append(
            pltpu.make_async_remote_copy(
                src_ref=source.at[n % 2],
                dst_ref=target.at[n % 2],
                send_sem=sent.at[n],
                recv_sem=came.at[n],
                device_id=neighbour(n),
                device_id_type=pl.DeviceIdType.MESH,
            )
        )
        copies[-1].start()
    for copy in copies:
        copy.wait()
    panel = lax.axis_index("panel")
    zero = jnp.zeros(above.shape, jnp.bfloat16)
    above[...] = jnp.where(panel > 0, row_in[0], zero)
    below[...] = jnp.where(panel < lax.axis_size("panel") - 1, row_in[1], zero)
    before[...] = col_in[0]
    after[...] = col_in[1]


def gather_kernel(
    count, cells, flux, above, below, before, after, weight, offset, pattern, out, wide, grid, mom
):
    fields, height, breadth = flux.shape
    members, capacity = cells.shape
    pitch = breadth + 2 * LEFT
    chunks = capacity // LANES
    shift = breadth.bit_length() - 1
    assert breadth == 1 << shift
    fill = jnp.zeros((LANES - fields, breadth), jnp.float32)

    grid[...] = jnp.zeros_like(grid)

    def widen(f, carry):
        wide[pl.ds(f * height, height), :] = flux[f].astype(jnp.float32)
        return carry

    lax.fori_loop(0, fields, widen, 0, unroll=8)

    def place(row, block):
        turned = jnp.concatenate([block, fill], axis=0).T
        grid[pl.ds(pl.multiple_of(row * pitch + LEFT, 8), breadth), :] = turned

    for r in range(2):
        place(r, above[r].astype(jnp.float32))
        place(height + 2 + r, below[r].astype(jnp.float32))

    def turn(i, carry):
        place(i + 2, wide[pl.ds(i, fields, stride=height), :])
        return carry

    lax.fori_loop(0, height, turn, 0, unroll=4)
    for q in range(2):
        grid[pl.ds(2 * pitch + LEFT - 2 + q, height, stride=pitch), :] = before[q].astype(jnp.float32)
        grid[pl.ds(2 * pitch + LEFT + breadth + q, height, stride=pitch), :] = after[q].astype(
            jnp.float32
        )

    w = weight[...]
    ox = offset[0]
    oy = offset[1]
    moments = [
        jnp.sum(w, axis=0),
        jnp.sum(w * ox, axis=0) / 12.0,
        jnp.sum(w * oy, axis=0) / 12.0,
        0.5 * jnp.sum(w * ox * ox, axis=0) / 12.0,
        0.5 * jnp.sum(w * oy * oy, axis=0) / 12.0,
    ]
    mom[...] = jnp.zeros_like(mom)
    slots = lax.broadcasted_iota(jnp.int32, (1, capacity), 1)
    alive = [slots < count[k] for k in range(members)]
    for m, moment in enumerate(moments):
        for part in range(PARTS):
            piece = moment.astype(jnp.bfloat16).astype(jnp.float32)
            moment = moment - piece
            for k in range(members):
                mom[k, part * 8 + m : part * 8 + m + 1, :] = jnp.where(alive[k], piece[k : k + 1, :], 0.0)

    slot_group = lax.broadcasted_iota(jnp.int32, (LANES, GROUP * TAPS), 0) % GROUP
    tap_group = lax.broadcasted_iota(jnp.int32, (LANES, GROUP * TAPS), 1) // TAPS
    diagonal = slot_group == tap_group

    def chunk(step, carry):
        k = step // chunks
        q = step % chunks
        start = pl.multiple_of(q * LANES, LANES)
        live = count[k] - start

        @pl.when(live > 0)
        def _():
            m = mom[k, :, pl.ds(start, LANES)].T.astype(jnp.bfloat16)
            coef = jnp.dot(m, pattern[...], preferred_element_type=jnp.float32)
            coef = jnp.where(diagonal, coef, 0.0)
            high = coef.astype(jnp.bfloat16)
            low = (coef - high.astype(jnp.float32)).astype(jnp.bfloat16)
            parts = []
            for g in range(LANES // GROUP):
                taps = []
                for s in range(GROUP):
                    cell = cells[k, start + g * GROUP + s]
                    base = cell + lax.shift_right_logical(cell, shift) * (pitch - breadth)
                    taps.append(grid[pl.ds(base + 2 * pitch + LEFT - 2, 8), :])
                    taps.append(grid[pl.ds(base + LEFT, 8, stride=pitch), :])
                picked = jnp.concatenate(taps, axis=0).astype(jnp.bfloat16)
                rows = slice(g * GROUP, (g + 1) * GROUP)
                both = jnp.concatenate([high[rows], low[rows]], axis=0)
                r = jnp.dot(both, picked, preferred_element_type=jnp.float32)
                parts.append(r[:GROUP] + r[GROUP:])
            record = jnp.concatenate(parts, axis=0).T
            out[k, :, pl.ds(start, LANES)] = record[:fields].astype(jnp.bfloat16)

        @pl.when(live <= 0)
        def _():
            out[k, :, pl.ds(start, LANES)] = jnp.zeros((fields, LANES), jnp.bfloat16)

        return carry

    lax.fori_loop(0, members * chunks, chunk, 0)


def scatter_kernel(records, target, area, out, landed, masked, total, sent, came):
    members, fields, capacity = records.shape
    digits = out.shape[1] // LOW
    rows = total.shape[0] // digits
    fill = jnp.zeros((rows - fields, capacity), jnp.bfloat16)
    me = lax.axis_index("blk")

    def peer(step):
        return {"blk": lax.rem(me + step, members)}

    def copy(step):
        return pltpu.make_async_remote_copy(
            src_ref=records.at[lax.rem(me + step, members)],
            dst_ref=landed.at[step - 1],
            send_sem=sent.at[step - 1],
            recv_sem=came.at[step - 1],
            device_id=peer(step),
            device_id_type=pl.DeviceIdType.MESH,
        )

    barrier = pltpu.get_barrier_semaphore()
    for step in range(1, members):
        pl.semaphore_signal(barrier, 1, device_id=peer(step), device_id_type=pl.DeviceIdType.MESH)
    pl.semaphore_wait(barrier, members - 1)
    for step in range(1, members):
        copy(step).start()

    def deposit(record, source):
        cell = target[pl.ds(source, 1), :]
        high = lax.shift_right_logical(cell, LOW.bit_length() - 1)
        low = cell & (LOW - 1)
        spots = lax.broadcasted_iota(jnp.int32, (LOW, capacity), 0)
        table = jnp.where(spots == low, 1.0, 0.0).astype(jnp.bfloat16)
        record = jnp.concatenate([record, fill], axis=0)
        for h in range(digits):
            here = jnp.where(high == h, 1.0, 0.0).astype(jnp.bfloat16)
            masked[h * rows : (h + 1) * rows, :] = record * here
        return lax.dot_general(
            masked[...], table, (((1,), (1,)), ((), ())), preferred_element_type=jnp.float32
        )

    total[...] = deposit(records[me], me)

    def arrival(step, carry):
        copy(step).wait_recv()
        total[...] += deposit(landed[step - 1], lax.rem(me - step + members, members))
        return carry

    lax.fori_loop(1, members, arrival, 0)
    for h in range(digits):
        columns = slice(h * LOW, (h + 1) * LOW)
        value = total[h * rows : h * rows + fields, :] / area[:, columns]
        out[:, columns] = value.astype(jnp.bfloat16)
    for step in range(1, members):
        copy(step).wait_send()


def on_device(
    source_flux, gauss_weight, gauss_offset, slot_count, source_cell, target_cell, target_area
):
    fields, height, breadth = source_flux.shape
    members, capacity = source_cell.shape
    ocean_cells = target_area.shape[0]
    pitch = breadth + 2 * LEFT

    vmem = pl.BlockSpec(memory_space=pltpu.VMEM)
    smem = pl.BlockSpec(memory_space=pltpu.SMEM)
    row_halo = jax.ShapeDtypeStruct((2, fields, breadth), jnp.bfloat16)
    col_halo = jax.ShapeDtypeStruct((2, height, LANES), jnp.bfloat16)
    above, below, before, after = pl.pallas_call(
        halo_kernel,
        out_shape=[row_halo, row_halo, col_halo, col_halo],
        in_specs=[vmem],
        out_specs=[vmem] * 4,
        scratch_shapes=[
            pltpu.VMEM((fields * height, breadth), jnp.float32),
            pltpu.VMEM((height * 8, LANES), jnp.float32),
            pltpu.VMEM((2, 2, fields, breadth), jnp.bfloat16),
            pltpu.VMEM((2, 2, height, LANES), jnp.bfloat16),
            pltpu.VMEM((2, 2, fields, breadth), jnp.bfloat16),
            pltpu.VMEM((2, 2, height, LANES), jnp.bfloat16),
            pltpu.SemaphoreType.DMA((4,)),
            pltpu.SemaphoreType.DMA((4,)),
        ],
        compiler_params=pltpu.CompilerParams(
            vmem_limit_bytes=48 * 2**20, collective_id=1, has_side_effects=True
        ),
        name="exchange_halos",
    )(source_flux)
    records = pl.pallas_call(
        gather_kernel,
        out_shape=jax.ShapeDtypeStruct((members, fields, capacity), jnp.bfloat16),
        in_specs=[smem, smem] + [vmem] * 8,
        out_specs=vmem,
        scratch_shapes=[
            pltpu.VMEM((fields * height, breadth), jnp.float32),
            pltpu.VMEM(((height + 8) * pitch, LANES), jnp.float32),
            pltpu.VMEM((members, 8 * PARTS, capacity), jnp.float32),
        ],
        compiler_params=pltpu.CompilerParams(vmem_limit_bytes=48 * 2**20),
        name="gather_records",
    )(
        slot_count,
        source_cell,
        source_flux,
        above,
        below,
        before,
        after,
        gauss_weight,
        gauss_offset,
        jnp.asarray(tap_pattern(), jnp.bfloat16),
    )
    digits = ocean_cells // LOW
    rows = -(-fields // 16) * 16
    return pl.pallas_call(
        scatter_kernel,
        out_shape=jax.ShapeDtypeStruct((fields, ocean_cells), jnp.bfloat16),
        in_specs=[vmem] * 3,
        out_specs=vmem,
        scratch_shapes=[
            pltpu.VMEM((members - 1, fields, capacity), jnp.bfloat16),
            pltpu.VMEM((digits * rows, capacity), jnp.bfloat16),
            pltpu.VMEM((digits * rows, LOW), jnp.float32),
            pltpu.SemaphoreType.DMA((members - 1,)),
            pltpu.SemaphoreType.DMA((members - 1,)),
        ],
        compiler_params=pltpu.CompilerParams(
            vmem_limit_bytes=48 * 2**20, collective_id=0, has_side_effects=True
        ),
        name="scatter_records",
    )(records, target_cell, target_area.reshape(1, ocean_cells))


def solution(mesh):
    placed = (
        P(None, "panel", "blk"),
        P(None, ("panel", "blk"), None),
        P(None, None, ("panel", "blk"), None),
        P(("panel", "blk")),
        P(("panel", "blk"), None),
        P(("panel", "blk"), None),
        P(("panel", "blk")),
    )
    return jax.shard_map(
        on_device, mesh=mesh, in_specs=placed, out_specs=P(None, ("panel", "blk")), check_vma=False
    )
```

```python
import jax
import jax.numpy as jnp
import numpy as np
from jax import lax
from jax.experimental import pallas as pl
from jax.experimental.pallas import tpu as pltpu
from jax.sharding import PartitionSpec as P

LANES = 128
GROUP = 16
TAPS = 16
LEFT = 8
PARTS = 3
LAG = 3
PAIR = 2
LOW = 256


def tap_pattern():
    first = np.array([1, -8, 0, 8, -1, 0, 0, 0])
    second = np.array([-1, 16, -30, 16, -1, 0, 0, 0])
    here = np.array([0, 0, 1, 0, 0, 0, 0, 0])
    none = np.zeros(8)
    rows = [
        np.concatenate([here, none]),
        np.concatenate([none, first]),
        np.concatenate([first, none]),
        np.concatenate([none, second]),
        np.concatenate([second, none]),
    ]
    rows += [np.zeros(TAPS)] * 3
    return np.tile(np.stack(rows), (PARTS, GROUP)).astype(np.float32)


def remap_kernel(
    count, cells, flux, weight, offset, pattern, targets, area, out,
    wide, grid, edges, mom, row_out, col_out, row_in, col_in, records, landed, masked, total,
    halo_sent, halo_came, sent, came,
):
    fields, height, breadth = flux.shape
    members, capacity = cells.shape
    pitch = breadth + 2 * LEFT
    chunks = capacity // LANES
    shift = breadth.bit_length() - 1
    assert breadth == 1 << shift
    digits = out.shape[1] // LOW
    rows = total.shape[0] // digits
    axes = ("panel", "panel", "blk", "blk")
    shifts = (1, -1, 1, -1)
    mesh_id = pl.DeviceIdType.MESH
    me = lax.axis_index("blk")

    def neighbour(n):
        size = lax.axis_size(axes[n])
        return {axes[n]: lax.rem(lax.axis_index(axes[n]) + shifts[n] + size, size)}

    def member(step):
        return lax.rem(me + step, members)

    barrier = pltpu.get_barrier_semaphore()
    for n in range(2):
        pl.semaphore_signal(barrier, 1, device_id=neighbour(n), device_id_type=mesh_id)
    for step in range(1, members):
        pl.semaphore_signal(barrier, 1, device_id={"blk": member(step)}, device_id_type=mesh_id)

    def widen(f, carry):
        wide[pl.ds(f * height, height), :] = flux[f].astype(jnp.float32)
        return carry

    lax.fori_loop(0, fields, widen, 0, unroll=8)
    for side, first in enumerate((height - 2, 0)):
        for r in range(2):
            row = wide[pl.ds(first + r, fields, stride=height), :]
            row_out[side, r] = row.astype(jnp.bfloat16)

    line = lax.broadcasted_iota(jnp.int32, (16, breadth), 0)
    column = lax.broadcasted_iota(jnp.int32, (16, breadth), 1)
    wanted = jnp.where(line < 2, breadth - 2 + line, line - 2)
    chosen = jnp.where((column == wanted) & (line < 4), 1.0, 0.0).astype(jnp.bfloat16)
    fill = jnp.zeros((LANES - fields, breadth), jnp.float32)

    def pick(i, carry):
        block = jnp.concatenate([wide[pl.ds(i, fields, stride=height), :], fill], axis=0)
        picked = lax.dot_general(
            chosen,
            block.astype(jnp.bfloat16),
            (((1,), (1,)), ((), ())),
            preferred_element_type=jnp.float32,
        )
        edges[pl.ds(pl.multiple_of(i * 8, 8), 8), :] = picked[:8]
        return carry

    lax.fori_loop(0, height, pick, 0, unroll=8)
    for side in range(2):
        for q in range(2):
            col = edges[pl.ds(2 * side + q, height, stride=8), :]
            col_out[side, q] = col.astype(jnp.bfloat16)

    pl.semaphore_wait(barrier, members + 1)
    halos = []
    for n in range(4):
        source, target = (row_out, row_in) if n < 2 else (col_out, col_in)
        halos.append(
            pltpu.make_async_remote_copy(
                src_ref=source.at[n % 2],
                dst_ref=target.at[n % 2],
                send_sem=halo_sent.at[n],
                recv_sem=halo_came.at[n],
                device_id=neighbour(n),
                device_id_type=mesh_id,
            )
        )
        halos[-1].start()

    total[...] = jnp.zeros_like(total)
    gap = jnp.zeros((LEFT, LANES), jnp.float32)
    grid[(height + 4) * pitch :, :] = jnp.zeros((4 * pitch, LANES), jnp.float32)

    def place(row, block):
        start = pl.multiple_of(row * pitch, 8)
        turned = jnp.concatenate([block, fill], axis=0).T
        grid[pl.ds(start, LEFT), :] = gap
        grid[pl.ds(start + LEFT, breadth), :] = turned
        grid[pl.ds(start + LEFT + breadth, LEFT), :] = gap

    def turn(i, carry):
        place(i + 2, wide[pl.ds(i, fields, stride=height), :])
        return carry

    lax.fori_loop(0, height, turn, 0, unroll=4)

    w = weight[...]
    ox = offset[0]
    oy = offset[1]
    moments = [
        jnp.sum(w, axis=0),
        jnp.sum(w * ox, axis=0) / 12.0,
        jnp.sum(w * oy, axis=0) / 12.0,
        0.5 * jnp.sum(w * ox * ox, axis=0) / 12.0,
        0.5 * jnp.sum(w * oy * oy, axis=0) / 12.0,
    ]
    mom[...] = jnp.zeros_like(mom)
    slots = lax.broadcasted_iota(jnp.int32, (1, capacity), 1)
    alive = [slots < count[k] for k in range(members)]
    for m, moment in enumerate(moments):
        for part in range(PARTS):
            piece = moment.astype(jnp.bfloat16).astype(jnp.float32)
            moment = moment - piece
            for k in range(members):
                mom[k, part * 8 + m : part * 8 + m + 1, :] = jnp.where(
                    alive[k], piece[k : k + 1, :], 0.0
                )

    for halo in halos:
        halo.wait()
    panel = lax.axis_index("panel")
    has_above = jnp.where(panel > 0, 1.0, 0.0)
    has_below = jnp.where(panel < lax.axis_size("panel") - 1, 1.0, 0.0)
    for r in range(2):
        place(r, row_in[0, r].astype(jnp.float32) * has_above)
        place(height + 2 + r, row_in[1, r].astype(jnp.float32) * has_below)
    for q in range(2):
        grid[pl.ds(2 * pitch + LEFT - 2 + q, height, stride=pitch), :] = col_in[0, q].astype(
            jnp.float32
        )
        grid[pl.ds(2 * pitch + LEFT + breadth + q, height, stride=pitch), :] = col_in[1, q].astype(
            jnp.float32
        )

    slot_group = lax.broadcasted_iota(jnp.int32, (LANES, GROUP * TAPS), 0) % GROUP
    tap_group = lax.broadcasted_iota(jnp.int32, (LANES, GROUP * TAPS), 1) // TAPS
    diagonal = slot_group == tap_group

    def gather(k, step, start):
        m = mom[k, :, pl.ds(start, LANES)].T.astype(jnp.bfloat16)
        coef = jnp.dot(m, pattern[...], preferred_element_type=jnp.float32)
        coef = jnp.where(diagonal, coef, 0.0)
        high = coef.astype(jnp.bfloat16)
        low = (coef - high.astype(jnp.float32)).astype(jnp.bfloat16)
        parts = []
        for g in range(LANES // GROUP):
            taps = []
            for s in range(GROUP):
                cell = cells[k, start + g * GROUP + s]
                base = cell + lax.shift_right_logical(cell, shift) * (pitch - breadth)
                taps.append(grid[pl.ds(base + 2 * pitch + LEFT - 2, 8), :])
                taps.append(grid[pl.ds(base + LEFT, 8, stride=pitch), :])
            picked = jnp.concatenate(taps, axis=0).astype(jnp.bfloat16)
            some = slice(g * GROUP, (g + 1) * GROUP)
            both = jnp.concatenate([high[some], low[some]], axis=0)
            r = jnp.dot(both, picked, preferred_element_type=jnp.float32)
            parts.append(r[:GROUP] + r[GROUP:])
        record = jnp.concatenate(parts, axis=0).T
        records[step - 1, :, pl.ds(start, LANES)] = record[:fields].astype(jnp.bfloat16)

    def send(step):
        return pltpu.make_async_remote_copy(
            src_ref=records.at[step - 1],
            dst_ref=landed.at[step - 1],
            send_sem=sent.at[step - 1],
            recv_sem=came.at[step - 1],
            device_id={"blk": member(step)},
            device_id_type=mesh_id,
        )

    rest = jnp.zeros((rows - fields, capacity), jnp.bfloat16)

    def deposit(record, source):
        cell = targets[pl.ds(source, 1), :]
        high = lax.shift_right_logical(cell, LOW.bit_length() - 1)
        low = cell & (LOW - 1)
        spots = lax.broadcasted_iota(jnp.int32, (LOW, capacity), 0)
        table = jnp.where(spots == low, 1.0, 0.0).astype(jnp.bfloat16)
        record = jnp.concatenate([record, rest], axis=0)
        for h in range(digits):
            here = jnp.where(high == h, 1.0, 0.0).astype(jnp.bfloat16)
            masked[h * rows : (h + 1) * rows, :] = record * here
        total[...] += lax.dot_general(
            masked[...], table, (((1,), (1,)), ((), ())), preferred_element_type=jnp.float32
        )

    def arrival(step, carry):
        send(step).wait_recv()
        deposit(landed[step - 1], lax.rem(me - step + members, members))
        return carry

    def advance(step, carry):
        def pair(p, inner):
            for c in range(PAIR):
                gather(member(step), step, pl.multiple_of((p * PAIR + c) * LANES, LANES))
            return inner

        lax.fori_loop(0, chunks // PAIR, pair, 0)

        @pl.when(step < members)
        def _():
            send(step).start()

        @pl.when(step > LAG)
        def _():
            arrival(step - LAG, 0)

        return carry

    lax.fori_loop(1, members + 1, advance, 0)
    deposit(records[members - 1], me)
    lax.fori_loop(members + 1 - LAG, members, arrival, 0)
    for h in range(digits):
        columns = slice(h * LOW, (h + 1) * LOW)
        value = total[h * rows : h * rows + fields, :] / area[:, columns]
        out[:, columns] = value.astype(jnp.bfloat16)

    def finish(step, carry):
        send(step).wait_send()
        return carry

    lax.fori_loop(1, members, finish, 0)


def on_device(
    source_flux, gauss_weight, gauss_offset, slot_count, source_cell, target_cell, target_area
):
    fields, height, breadth = source_flux.shape
    members, capacity = source_cell.shape
    ocean_cells = target_area.shape[0]
    pitch = breadth + 2 * LEFT
    digits = ocean_cells // LOW
    rows = -(-fields // 16) * 16
    vmem = pl.BlockSpec(memory_space=pltpu.VMEM)
    smem = pl.BlockSpec(memory_space=pltpu.SMEM)
    return pl.pallas_call(
        remap_kernel,
        out_shape=jax.ShapeDtypeStruct((fields, ocean_cells), jnp.bfloat16),
        in_specs=[smem, smem] + [vmem] * 6,
        out_specs=vmem,
        scratch_shapes=[
            pltpu.VMEM((fields * height, breadth), jnp.float32),
            pltpu.VMEM(((height + 8) * pitch, LANES), jnp.float32),
            pltpu.VMEM((height * 8, LANES), jnp.float32),
            pltpu.VMEM((members, 8 * PARTS, capacity), jnp.float32),
            pltpu.VMEM((2, 2, fields, breadth), jnp.bfloat16),
            pltpu.VMEM((2, 2, height, LANES), jnp.bfloat16),
            pltpu.VMEM((2, 2, fields, breadth), jnp.bfloat16),
            pltpu.VMEM((2, 2, height, LANES), jnp.bfloat16),
            pltpu.VMEM((members, fields, capacity), jnp.bfloat16),
            pltpu.VMEM((members - 1, fields, capacity), jnp.bfloat16),
            pltpu.VMEM((digits * rows, capacity), jnp.bfloat16),
            pltpu.VMEM((digits * rows, LOW), jnp.float32),
            pltpu.SemaphoreType.DMA((4,)),
            pltpu.SemaphoreType.DMA((4,)),
            pltpu.SemaphoreType.DMA((members - 1,)),
            pltpu.SemaphoreType.DMA((members - 1,)),
        ],
        compiler_params=pltpu.CompilerParams(
            vmem_limit_bytes=48 * 2**20, collective_id=0, has_side_effects=True
        ),
        name="remap",
    )(
        slot_count,
        source_cell,
        source_flux,
        gauss_weight,
        gauss_offset,
        jnp.asarray(tap_pattern(), jnp.bfloat16),
        target_cell,
        target_area.reshape(1, ocean_cells),
    )


def solution(mesh):
    placed = (
        P(None, "panel", "blk"),
        P(None, ("panel", "blk"), None),
        P(None, None, ("panel", "blk"), None),
        P(("panel", "blk")),
        P(("panel", "blk"), None),
        P(("panel", "blk"), None),
        P(("panel", "blk")),
    )
    return jax.shard_map(
        on_device, mesh=mesh, in_specs=placed, out_specs=P(None, ("panel", "blk")), check_vma=False
    )
```

```python
import jax
import jax.numpy as jnp
import numpy as np
from jax import lax
from jax.experimental import pallas as pl
from jax.experimental.pallas import tpu as pltpu
from jax.sharding import PartitionSpec as P

LANES = 128
GROUP = 16
TAPS = 16
LEFT = 8
PARTS = 3
LAG = 3
PAIR = 2
LOW = 256


def tap_pattern():
    first = np.array([1, -8, 0, 8, -1, 0, 0, 0])
    second = np.array([-1, 16, -30, 16, -1, 0, 0, 0])
    here = np.array([0, 0, 1, 0, 0, 0, 0, 0])
    none = np.zeros(8)
    rows = [
        np.concatenate([here, none]),
        np.concatenate([none, first]),
        np.concatenate([first, none]),
        np.concatenate([none, second]),
        np.concatenate([second, none]),
    ]
    rows += [np.zeros(TAPS)] * 3
    return np.tile(np.stack(rows), (PARTS, GROUP)).astype(np.float32)


def remap_kernel(
    count, hbm_cells, hbm_flux, hbm_weight, hbm_offset, hbm_pattern, hbm_targets, hbm_area, out,
    cells, flux, weight, offset, pattern, targets, area, loaded, wide, grid, edges, mom, row_out, col_out, row_in, col_in, records, landed, masked, total,
    halo_sent, halo_came, sent, came,
):
    fields, height, breadth = flux.shape
    members, capacity = cells.shape
    pitch = breadth + 2 * LEFT + 1
    deep = height + 1
    chunks = capacity // LANES
    shift = breadth.bit_length() - 1
    assert breadth == 1 << shift
    digits = out.shape[1] // LOW
    rows = total.shape[0] // digits
    axes = ("panel", "panel", "blk", "blk")
    shifts = (1, -1, 1, -1)
    mesh_id = pl.DeviceIdType.MESH
    me = lax.axis_index("blk")

    def neighbour(n):
        size = lax.axis_size(axes[n])
        return {axes[n]: lax.rem(lax.axis_index(axes[n]) + shifts[n] + size, size)}

    def member(step):
        return lax.rem(me + step, members)

    loads = [
        pltpu.make_async_copy(source, target, loaded.at[n])
        for n, (source, target) in enumerate(
            (
                (hbm_flux, flux),
                (hbm_weight, weight),
                (hbm_offset, offset),
                (hbm_pattern, pattern),
                (hbm_cells, cells),
                (hbm_targets, targets),
                (hbm_area, area),
            )
        )
    ]
    for load in loads:
        load.start()
    barrier = pltpu.get_barrier_semaphore()
    for n in range(2):
        pl.semaphore_signal(barrier, 1, device_id=neighbour(n), device_id_type=mesh_id)
    for step in range(1, members):
        pl.semaphore_signal(barrier, 1, device_id={"blk": member(step)}, device_id_type=mesh_id)

    def widen(f, carry):
        wide[pl.ds(f * deep, height), :] = flux[f].astype(jnp.float32)
        return carry

    loads[0].wait()
    lax.fori_loop(0, fields, widen, 0, unroll=8)
    for side, first in enumerate((height - 2, 0)):
        for r in range(2):
            row = wide[pl.ds(first + r, fields, stride=deep), :]
            row_out[side, r] = row.astype(jnp.bfloat16)

    line = lax.broadcasted_iota(jnp.int32, (16, breadth), 0)
    column = lax.broadcasted_iota(jnp.int32, (16, breadth), 1)
    wanted = jnp.where(line < 2, breadth - 2 + line, line - 2)
    chosen = jnp.where((column == wanted) & (line < 4), 1.0, 0.0).astype(jnp.bfloat16)
    fill = jnp.zeros((LANES - fields, breadth), jnp.float32)

    def pick(i, carry):
        block = jnp.concatenate([wide[pl.ds(i, fields, stride=deep), :], fill], axis=0)
        picked = lax.dot_general(
            chosen,
            block.astype(jnp.bfloat16),
            (((1,), (1,)), ((), ())),
            preferred_element_type=jnp.float32,
        )
        edges[pl.ds(pl.multiple_of(i * 8, 8), 8), :] = picked[:8]
        return carry

    lax.fori_loop(0, height, pick, 0, unroll=8)
    for side in range(2):
        for q in range(2):
            col = edges[pl.ds(2 * side + q, height, stride=8), :]
            col_out[side, q] = col.astype(jnp.bfloat16)

    pl.semaphore_wait(barrier, members + 1)
    halos = []
    for n in range(4):
        source, target = (row_out, row_in) if n < 2 else (col_out, col_in)
        halos.append(
            pltpu.make_async_remote_copy(
                src_ref=source.at[n % 2],
                dst_ref=target.at[n % 2],
                send_sem=halo_sent.at[n],
                recv_sem=halo_came.at[n],
                device_id=neighbour(n),
                device_id_type=mesh_id,
            )
        )
        halos[-1].start()

    total[...] = jnp.zeros_like(total)
    gap = jnp.zeros((LEFT, LANES), jnp.float32)
    grid[(height + 4) * pitch :, :] = jnp.zeros((4 * pitch, LANES), jnp.float32)

    def place(row, block):
        start = row * pitch
        turned = jnp.concatenate([block, fill], axis=0).T
        grid[pl.ds(start, LEFT), :] = gap
        grid[pl.ds(start + LEFT, breadth), :] = turned
        grid[pl.ds(start + LEFT + breadth, LEFT), :] = gap

    def turn(i, carry):
        place(i + 2, wide[pl.ds(i, fields, stride=deep), :])
        return carry

    lax.fori_loop(0, height, turn, 0, unroll=4)

    for load in loads[1:]:
        load.wait()
    w = weight[...]
    ox = offset[0]
    oy = offset[1]
    moments = [
        jnp.sum(w, axis=0),
        jnp.sum(w * ox, axis=0) / 12.0,
        jnp.sum(w * oy, axis=0) / 12.0,
        0.5 * jnp.sum(w * ox * ox, axis=0) / 12.0,
        0.5 * jnp.sum(w * oy * oy, axis=0) / 12.0,
    ]
    mom[...] = jnp.zeros_like(mom)
    slots = lax.broadcasted_iota(jnp.int32, (1, capacity), 1)
    alive = [slots < count[k] for k in range(members)]
    for m, moment in enumerate(moments):
        for part in range(PARTS):
            piece = moment.astype(jnp.bfloat16).astype(jnp.float32)
            moment = moment - piece
            for k in range(members):
                mom[k, part * 8 + m : part * 8 + m + 1, :] = jnp.where(
                    alive[k], piece[k : k + 1, :], 0.0
                )

    for halo in halos:
        halo.wait()
    panel = lax.axis_index("panel")
    has_above = jnp.where(panel > 0, 1.0, 0.0)
    has_below = jnp.where(panel < lax.axis_size("panel") - 1, 1.0, 0.0)
    for r in range(2):
        place(r, row_in[0, r].astype(jnp.float32) * has_above)
        place(height + 2 + r, row_in[1, r].astype(jnp.float32) * has_below)
    for q in range(2):
        grid[pl.ds(2 * pitch + LEFT - 2 + q, height, stride=pitch), :] = col_in[0, q].astype(
            jnp.float32
        )
        grid[pl.ds(2 * pitch + LEFT + breadth + q, height, stride=pitch), :] = col_in[1, q].astype(
            jnp.float32
        )

    slot_group = lax.broadcasted_iota(jnp.int32, (LANES, GROUP * TAPS), 0) % GROUP
    tap_group = lax.broadcasted_iota(jnp.int32, (LANES, GROUP * TAPS), 1) // TAPS
    diagonal = slot_group == tap_group

    def gather(k, step, start):
        m = mom[k, :, pl.ds(start, LANES)].T.astype(jnp.bfloat16)
        coef = jnp.dot(m, pattern[...], preferred_element_type=jnp.float32)
        coef = jnp.where(diagonal, coef, 0.0)
        high = coef.astype(jnp.bfloat16)
        low = (coef - high.astype(jnp.float32)).astype(jnp.bfloat16)
        parts = []
        for g in range(LANES // GROUP):
            taps = []
            for s in range(GROUP):
                cell = cells[k, start + g * GROUP + s]
                base = cell + lax.shift_right_logical(cell, shift) * (pitch - breadth)
                taps.append(grid[pl.ds(base + 2 * pitch + LEFT - 2, 8), :])
                taps.append(grid[pl.ds(base + LEFT, 8, stride=pitch), :])
            picked = jnp.concatenate(taps, axis=0).astype(jnp.bfloat16)
            some = slice(g * GROUP, (g + 1) * GROUP)
            both = jnp.concatenate([high[some], low[some]], axis=0)
            r = jnp.dot(both, picked, preferred_element_type=jnp.float32)
            parts.append(r[:GROUP] + r[GROUP:])
        record = jnp.concatenate(parts, axis=0).T
        records[step - 1, :, pl.ds(start, LANES)] = record[:fields].astype(jnp.bfloat16)

    def send(step):
        return pltpu.make_async_remote_copy(
            src_ref=records.at[step - 1],
            dst_ref=landed.at[step - 1],
            send_sem=sent.at[step - 1],
            recv_sem=came.at[step - 1],
            device_id={"blk": member(step)},
            device_id_type=mesh_id,
        )

    rest = jnp.zeros((rows - fields, capacity), jnp.bfloat16)

    def deposit(record, source):
        cell = targets[pl.ds(source, 1), :]
        high = lax.shift_right_logical(cell, LOW.bit_length() - 1)
        low = cell & (LOW - 1)
        spots = lax.broadcasted_iota(jnp.int32, (LOW, capacity), 0)
        table = jnp.where(spots == low, 1.0, 0.0).astype(jnp.bfloat16)
        record = jnp.concatenate([record, rest], axis=0)
        for h in range(digits):
            here = jnp.where(high == h, 1.0, 0.0).astype(jnp.bfloat16)
            masked[h * rows : (h + 1) * rows, :] = record * here
        total[...] += lax.dot_general(
            masked[...], table, (((1,), (1,)), ((), ())), preferred_element_type=jnp.float32
        )

    def arrival(step, carry):
        send(step).wait_recv()
        deposit(landed[step - 1], lax.rem(me - step + members, members))
        return carry

    def advance(step, carry):
        def pair(p, inner):
            for c in range(PAIR):
                gather(member(step), step, pl.multiple_of((p * PAIR + c) * LANES, LANES))
            return inner

        lax.fori_loop(0, chunks // PAIR, pair, 0)

        @pl.when(step < members)
        def _():
            send(step).start()

        @pl.when(step > LAG)
        def _():
            arrival(step - LAG, 0)

        return carry

    lax.fori_loop(1, members + 1, advance, 0)
    deposit(records[members - 1], me)
    lax.fori_loop(members + 1 - LAG, members, arrival, 0)
    for h in range(digits):
        columns = slice(h * LOW, (h + 1) * LOW)
        value = total[h * rows : h * rows + fields, :] / area[:, columns]
        out[:, columns] = value.astype(jnp.bfloat16)

    def finish(step, carry):
        send(step).wait_send()
        return carry

    lax.fori_loop(1, members, finish, 0)


def on_device(
    source_flux, gauss_weight, gauss_offset, slot_count, source_cell, target_cell, target_area
):
    fields, height, breadth = source_flux.shape
    members, capacity = source_cell.shape
    ocean_cells = target_area.shape[0]
    pitch = breadth + 2 * LEFT + 1
    digits = ocean_cells // LOW
    rows = -(-fields // 16) * 16
    vmem = pl.BlockSpec(memory_space=pltpu.VMEM)
    smem = pl.BlockSpec(memory_space=pltpu.SMEM)
    hbm = pl.BlockSpec(memory_space=pltpu.HBM)
    pattern = jnp.asarray(tap_pattern(), jnp.bfloat16)
    return pl.pallas_call(
        remap_kernel,
        out_shape=jax.ShapeDtypeStruct((fields, ocean_cells), jnp.bfloat16),
        in_specs=[smem] + [hbm] * 7,
        out_specs=vmem,
        scratch_shapes=[
            pltpu.SMEM(source_cell.shape, jnp.int32),
            pltpu.VMEM(source_flux.shape, jnp.bfloat16),
            pltpu.VMEM(gauss_weight.shape, jnp.float32),
            pltpu.VMEM(gauss_offset.shape, jnp.float32),
            pltpu.VMEM(pattern.shape, jnp.bfloat16),
            pltpu.VMEM(target_cell.shape, jnp.int32),
            pltpu.VMEM((1, ocean_cells), jnp.float32),
            pltpu.SemaphoreType.DMA((7,)),
            pltpu.VMEM((fields * (height + 1), breadth), jnp.float32),
            pltpu.VMEM(((height + 8) * pitch, LANES), jnp.float32),
            pltpu.VMEM((height * 8, LANES), jnp.float32),
            pltpu.VMEM((members, 8 * PARTS, capacity), jnp.float32),
            pltpu.VMEM((2, 2, fields, breadth), jnp.bfloat16),
            pltpu.VMEM((2, 2, height, LANES), jnp.bfloat16),
            pltpu.VMEM((2, 2, fields, breadth), jnp.bfloat16),
            pltpu.VMEM((2, 2, height, LANES), jnp.bfloat16),
            pltpu.VMEM((members, fields, capacity), jnp.bfloat16),
            pltpu.VMEM((members - 1, fields, capacity), jnp.bfloat16),
            pltpu.VMEM((digits * rows, capacity), jnp.bfloat16),
            pltpu.VMEM((digits * rows, LOW), jnp.float32),
            pltpu.SemaphoreType.DMA((4,)),
            pltpu.SemaphoreType.DMA((4,)),
            pltpu.SemaphoreType.DMA((members - 1,)),
            pltpu.SemaphoreType.DMA((members - 1,)),
        ],
        compiler_params=pltpu.CompilerParams(
            vmem_limit_bytes=63 * 2**20, collective_id=0, has_side_effects=True
        ),
        name="remap",
    )(
        slot_count,
        source_cell,
        source_flux,
        gauss_weight,
        gauss_offset,
        pattern,
        target_cell,
        target_area.reshape(1, ocean_cells),
    )


def solution(mesh):
    placed = (
        P(None, "panel", "blk"),
        P(None, ("panel", "blk"), None),
        P(None, None, ("panel", "blk"), None),
        P(("panel", "blk")),
        P(("panel", "blk"), None),
        P(("panel", "blk"), None),
        P(("panel", "blk")),
    )
    return jax.shard_map(
        on_device, mesh=mesh, in_specs=placed, out_specs=P(None, ("panel", "blk")), check_vma=False
    )
```

```python
import jax
import jax.numpy as jnp
import numpy as np
from jax import lax
from jax.experimental import pallas as pl
from jax.experimental.pallas import tpu as pltpu
from jax.sharding import PartitionSpec as P

LANES = 128
GROUP = 16
TAPS = 16
LEFT = 8
PARTS = 3
LAG = 3
PAIR = 2
LOW = 256


def tap_pattern():
    first = np.array([1, -8, 0, 8, -1, 0, 0, 0])
    second = np.array([-1, 16, -30, 16, -1, 0, 0, 0])
    here = np.array([0, 0, 1, 0, 0, 0, 0, 0])
    none = np.zeros(8)
    rows = [
        np.concatenate([here, none]),
        np.concatenate([none, first]),
        np.concatenate([first, none]),
        np.concatenate([none, second]),
        np.concatenate([second, none]),
    ]
    rows += [np.zeros(TAPS)] * 3
    return np.tile(np.stack(rows), (PARTS, GROUP)).astype(np.float32)


def remap_kernel(
    count, hbm_cells, hbm_flux, hbm_weight, hbm_offset, hbm_pattern, hbm_targets, out,
    cells, bases, places, flux, weight, offset, pattern, targets, loaded, placed, wide, grid, edges, mom, row_out, col_out, row_in, col_in, records, landed, masked, total,
    halo_sent, halo_came, sent, came,
):
    fields, height, breadth = flux.shape
    members, capacity = cells.shape
    pitch = breadth + 2 * LEFT + 1
    deep = height + 1
    chunks = capacity // LANES
    shift = breadth.bit_length() - 1
    assert breadth == 1 << shift
    digits = out.shape[1] // LOW
    rows = total.shape[0] // digits
    axes = ("panel", "panel", "blk", "blk")
    shifts = (1, -1, 1, -1)
    mesh_id = pl.DeviceIdType.MESH
    me = lax.axis_index("blk")

    def neighbour(n):
        size = lax.axis_size(axes[n])
        return {axes[n]: lax.rem(lax.axis_index(axes[n]) + shifts[n] + size, size)}

    def member(step):
        return lax.rem(me + step, members)

    loads = [
        pltpu.make_async_copy(source, target, loaded.at[n])
        for n, (source, target) in enumerate(
            (
                (hbm_flux, flux),
                (hbm_weight, weight),
                (hbm_offset, offset),
                (hbm_pattern, pattern),
                (hbm_cells, cells),
                (hbm_targets, targets),
            )
        )
    ]
    for load in loads:
        load.start()
    barrier = pltpu.get_barrier_semaphore()
    for n in range(2):
        pl.semaphore_signal(barrier, 1, device_id=neighbour(n), device_id_type=mesh_id)
    for step in range(1, members):
        pl.semaphore_signal(barrier, 1, device_id={"blk": member(step)}, device_id_type=mesh_id)

    def widen(f, carry):
        wide[pl.ds(f * deep, height), :] = flux[f].astype(jnp.float32)
        return carry

    loads[0].wait()
    lax.fori_loop(0, fields, widen, 0, unroll=8)
    for side, first in enumerate((height - 2, 0)):
        for r in range(2):
            row = wide[pl.ds(first + r, fields, stride=deep), :]
            row_out[side, r] = row.astype(jnp.bfloat16)

    line = lax.broadcasted_iota(jnp.int32, (16, breadth), 0)
    column = lax.broadcasted_iota(jnp.int32, (16, breadth), 1)
    wanted = jnp.where(line < 2, breadth - 2 + line, line - 2)
    chosen = jnp.where((column == wanted) & (line < 4), 1.0, 0.0).astype(jnp.bfloat16)
    fill = jnp.zeros((LANES - fields, breadth), jnp.float32)

    def pick(i, carry):
        block = jnp.concatenate([wide[pl.ds(i, fields, stride=deep), :], fill], axis=0)
        picked = lax.dot_general(
            chosen,
            block.astype(jnp.bfloat16),
            (((1,), (1,)), ((), ())),
            preferred_element_type=jnp.float32,
        )
        edges[pl.ds(pl.multiple_of(i * 8, 8), 8), :] = picked[:8]
        return carry

    lax.fori_loop(0, height, pick, 0, unroll=8)
    for side in range(2):
        for q in range(2):
            col = edges[pl.ds(2 * side + q, height, stride=8), :]
            col_out[side, q] = col.astype(jnp.bfloat16)

    pl.semaphore_wait(barrier, members + 1)
    halos = []
    for n in range(4):
        source, target = (row_out, row_in) if n < 2 else (col_out, col_in)
        halos.append(
            pltpu.make_async_remote_copy(
                src_ref=source.at[n % 2],
                dst_ref=target.at[n % 2],
                send_sem=halo_sent.at[n],
                recv_sem=halo_came.at[n],
                device_id=neighbour(n),
                device_id_type=mesh_id,
            )
        )
        halos[-1].start()

    total[...] = jnp.zeros_like(total)
    gap = jnp.zeros((LEFT, LANES), jnp.float32)
    grid[(height + 4) * pitch :, :] = jnp.zeros((4 * pitch, LANES), jnp.float32)

    def place(row, block):
        start = row * pitch
        turned = jnp.concatenate([block, fill], axis=0).T
        grid[pl.ds(start, LEFT), :] = gap
        grid[pl.ds(start + LEFT, breadth), :] = turned
        grid[pl.ds(start + LEFT + breadth, LEFT), :] = gap

    def turn(i, carry):
        place(i + 2, wide[pl.ds(i, fields, stride=deep), :])
        return carry

    lax.fori_loop(0, height, turn, 0, unroll=4)

    for load in loads[1:]:
        load.wait()
    cell = cells[...]
    bases[...] = cell + lax.shift_right_logical(cell, shift) * (pitch - breadth)
    placing = pltpu.make_async_copy(bases, places, placed)
    placing.start()
    w = weight[...]
    ox = offset[0]
    oy = offset[1]
    moments = [
        jnp.sum(w, axis=0),
        jnp.sum(w * ox, axis=0) / 12.0,
        jnp.sum(w * oy, axis=0) / 12.0,
        0.5 * jnp.sum(w * ox * ox, axis=0) / 12.0,
        0.5 * jnp.sum(w * oy * oy, axis=0) / 12.0,
    ]
    mom[...] = jnp.zeros_like(mom)
    slots = lax.broadcasted_iota(jnp.int32, (1, capacity), 1)
    alive = [slots < count[k] for k in range(members)]
    for m, moment in enumerate(moments):
        for part in range(PARTS):
            piece = moment.astype(jnp.bfloat16).astype(jnp.float32)
            moment = moment - piece
            for k in range(members):
                mom[k, part * 8 + m : part * 8 + m + 1, :] = jnp.where(
                    alive[k], piece[k : k + 1, :], 0.0
                )

    placing.wait()
    for halo in halos:
        halo.wait()
    panel = lax.axis_index("panel")
    has_above = jnp.where(panel > 0, 1.0, 0.0)
    has_below = jnp.where(panel < lax.axis_size("panel") - 1, 1.0, 0.0)
    for r in range(2):
        place(r, row_in[0, r].astype(jnp.float32) * has_above)
        place(height + 2 + r, row_in[1, r].astype(jnp.float32) * has_below)
    for q in range(2):
        grid[pl.ds(2 * pitch + LEFT - 2 + q, height, stride=pitch), :] = col_in[0, q].astype(
            jnp.float32
        )
        grid[pl.ds(2 * pitch + LEFT + breadth + q, height, stride=pitch), :] = col_in[1, q].astype(
            jnp.float32
        )

    slot_group = lax.broadcasted_iota(jnp.int32, (LANES, GROUP * TAPS), 0) % GROUP
    tap_group = lax.broadcasted_iota(jnp.int32, (LANES, GROUP * TAPS), 1) // TAPS
    diagonal = slot_group == tap_group

    def gather(k, step, start):
        m = mom[k, :, pl.ds(start, LANES)].T.astype(jnp.bfloat16)
        coef = jnp.dot(m, pattern[...], preferred_element_type=jnp.float32)
        coef = jnp.where(diagonal, coef, 0.0)
        high = coef.astype(jnp.bfloat16)
        low = (coef - high.astype(jnp.float32)).astype(jnp.bfloat16)
        parts = []
        for g in range(LANES // GROUP):
            taps = []
            for s in range(GROUP):
                base = places[k, start + g * GROUP + s]
                taps.append(grid[pl.ds(base + 2 * pitch + LEFT - 2, 8), :])
                taps.append(grid[pl.ds(base + LEFT, 8, stride=pitch), :])
            picked = jnp.concatenate(taps, axis=0).astype(jnp.bfloat16)
            some = slice(g * GROUP, (g + 1) * GROUP)
            both = jnp.concatenate([high[some], low[some]], axis=0)
            r = jnp.dot(both, picked, preferred_element_type=jnp.float32)
            parts.append(r[:GROUP] + r[GROUP:])
        record = jnp.concatenate(parts, axis=0).T
        records[step - 1, :, pl.ds(start, LANES)] = record[:fields].astype(jnp.bfloat16)

    def send(step):
        return pltpu.make_async_remote_copy(
            src_ref=records.at[step - 1],
            dst_ref=landed.at[step - 1],
            send_sem=sent.at[step - 1],
            recv_sem=came.at[step - 1],
            device_id={"blk": member(step)},
            device_id_type=mesh_id,
        )

    rest = jnp.zeros((rows - fields, capacity), jnp.bfloat16)

    def deposit(record, source):
        cell = targets[pl.ds(source, 1), :]
        high = lax.shift_right_logical(cell, LOW.bit_length() - 1)
        low = cell & (LOW - 1)
        spots = lax.broadcasted_iota(jnp.int32, (LOW, capacity), 0)
        table = jnp.where(spots == low, 1.0, 0.0).astype(jnp.bfloat16)
        record = jnp.concatenate([record, rest], axis=0)
        for h in range(digits):
            here = jnp.where(high == h, 1.0, 0.0).astype(jnp.bfloat16)
            masked[h * rows : (h + 1) * rows, :] = record * here
        total[...] += lax.dot_general(
            masked[...], table, (((1,), (1,)), ((), ())), preferred_element_type=jnp.float32
        )

    def arrival(step, carry):
        send(step).wait_recv()
        deposit(landed[step - 1], lax.rem(me - step + members, members))
        return carry

    def advance(step, carry):
        def pair(p, inner):
            for c in range(PAIR):
                gather(member(step), step, pl.multiple_of((p * PAIR + c) * LANES, LANES))
            return inner

        lax.fori_loop(0, chunks // PAIR, pair, 0)

        @pl.when(step < members)
        def _():
            send(step).start()

        @pl.when(step > LAG)
        def _():
            arrival(step - LAG, 0)

        return carry

    lax.fori_loop(1, members + 1, advance, 0)
    deposit(records[members - 1], me)
    lax.fori_loop(members + 1 - LAG, members, arrival, 0)
    for h in range(digits):
        columns = slice(h * LOW, (h + 1) * LOW)
        out[:, columns] = total[h * rows : h * rows + fields, :]

    def finish(step, carry):
        send(step).wait_send()
        return carry

    lax.fori_loop(1, members, finish, 0)


def on_device(
    source_flux, gauss_weight, gauss_offset, slot_count, source_cell, target_cell, target_area
):
    fields, height, breadth = source_flux.shape
    members, capacity = source_cell.shape
    ocean_cells = target_area.shape[0]
    pitch = breadth + 2 * LEFT + 1
    digits = ocean_cells // LOW
    rows = -(-fields // 16) * 16
    vmem = pl.BlockSpec(memory_space=pltpu.VMEM)
    smem = pl.BlockSpec(memory_space=pltpu.SMEM)
    hbm = pl.BlockSpec(memory_space=pltpu.HBM)
    pattern = jnp.asarray(tap_pattern(), jnp.bfloat16)
    integrated = pl.pallas_call(
        remap_kernel,
        out_shape=jax.ShapeDtypeStruct((fields, ocean_cells), jnp.float32),
        in_specs=[smem] + [hbm] * 6,
        out_specs=vmem,
        scratch_shapes=[
            pltpu.VMEM(source_cell.shape, jnp.int32),
            pltpu.VMEM(source_cell.shape, jnp.int32),
            pltpu.SMEM(source_cell.shape, jnp.int32),
            pltpu.VMEM(source_flux.shape, jnp.bfloat16),
            pltpu.VMEM(gauss_weight.shape, jnp.float32),
            pltpu.VMEM(gauss_offset.shape, jnp.float32),
            pltpu.VMEM(pattern.shape, jnp.bfloat16),
            pltpu.VMEM(target_cell.shape, jnp.int32),
            pltpu.SemaphoreType.DMA((6,)),
            pltpu.SemaphoreType.DMA,
            pltpu.VMEM((fields * (height + 1), breadth), jnp.float32),
            pltpu.VMEM(((height + 8) * pitch, LANES), jnp.float32),
            pltpu.VMEM((height * 8, LANES), jnp.float32),
            pltpu.VMEM((members, 8 * PARTS, capacity), jnp.float32),
            pltpu.VMEM((2, 2, fields, breadth), jnp.bfloat16),
            pltpu.VMEM((2, 2, height, LANES), jnp.bfloat16),
            pltpu.VMEM((2, 2, fields, breadth), jnp.bfloat16),
            pltpu.VMEM((2, 2, height, LANES), jnp.bfloat16),
            pltpu.VMEM((members, fields, capacity), jnp.bfloat16),
            pltpu.VMEM((members - 1, fields, capacity), jnp.bfloat16),
            pltpu.VMEM((digits * rows, capacity), jnp.bfloat16),
            pltpu.VMEM((digits * rows, LOW), jnp.float32),
            pltpu.SemaphoreType.DMA((4,)),
            pltpu.SemaphoreType.DMA((4,)),
            pltpu.SemaphoreType.DMA((members - 1,)),
            pltpu.SemaphoreType.DMA((members - 1,)),
        ],
        compiler_params=pltpu.CompilerParams(
            vmem_limit_bytes=63 * 2**20, collective_id=0, has_side_effects=True
        ),
        name="remap",
    )(
        slot_count,
        source_cell,
        source_flux,
        gauss_weight,
        gauss_offset,
        pattern,
        target_cell,
    )
    return (integrated / target_area[None, :]).astype(jnp.bfloat16)


def solution(mesh):
    placed = (
        P(None, "panel", "blk"),
        P(None, ("panel", "blk"), None),
        P(None, None, ("panel", "blk"), None),
        P(("panel", "blk")),
        P(("panel", "blk"), None),
        P(("panel", "blk"), None),
        P(("panel", "blk")),
    )
    return jax.shard_map(
        on_device, mesh=mesh, in_specs=placed, out_specs=P(None, ("panel", "blk")), check_vma=False
    )
```

```python
import jax
import jax.numpy as jnp
import numpy as np
from jax import lax
from jax.experimental import pallas as pl
from jax.experimental.pallas import tpu as pltpu
from jax.sharding import PartitionSpec as P

LANES = 128
GROUP = 16
TAPS = 16
LEFT = 8
PARTS = 3
LAG = 3
PAIR = 4
LOW = 256


def tap_pattern():
    first = np.array([1, -8, 0, 8, -1, 0, 0, 0])
    second = np.array([-1, 16, -30, 16, -1, 0, 0, 0])
    here = np.array([0, 0, 1, 0, 0, 0, 0, 0])
    none = np.zeros(8)
    rows = [
        np.concatenate([here, none]),
        np.concatenate([none, first]),
        np.concatenate([first, none]),
        np.concatenate([none, second]),
        np.concatenate([second, none]),
    ]
    rows += [np.zeros(TAPS)] * 3
    return np.tile(np.stack(rows), (PARTS, GROUP)).astype(np.float32)


def remap_kernel(
    count, hbm_cells, hbm_flux, hbm_weight, hbm_offset, hbm_pattern, hbm_targets, out,
    cells, bases, places, flux, weight, offset, pattern, targets, loaded, placed, wide, grid, edges, mom, row_out, col_out, row_in, col_in, records, landed, masked, total,
    halo_sent, halo_came, sent, came,
):
    fields, height, breadth = flux.shape
    members, capacity = cells.shape
    pitch = breadth + 2 * LEFT + 1
    deep = height + 1
    chunks = capacity // LANES
    shift = breadth.bit_length() - 1
    assert breadth == 1 << shift
    digits = out.shape[1] // LOW
    rows = total.shape[0] // digits
    axes = ("panel", "panel", "blk", "blk")
    shifts = (1, -1, 1, -1)
    mesh_id = pl.DeviceIdType.MESH
    me = lax.axis_index("blk")

    def neighbour(n):
        size = lax.axis_size(axes[n])
        return {axes[n]: lax.rem(lax.axis_index(axes[n]) + shifts[n] + size, size)}

    def member(step):
        return lax.rem(me + step, members)

    loads = [
        pltpu.make_async_copy(source, target, loaded.at[n])
        for n, (source, target) in enumerate(
            (
                (hbm_flux, flux),
                (hbm_weight, weight),
                (hbm_offset, offset),
                (hbm_pattern, pattern),
                (hbm_cells, cells),
                (hbm_targets, targets),
            )
        )
    ]
    for load in loads:
        load.start()
    barrier = pltpu.get_barrier_semaphore()
    for n in range(2):
        pl.semaphore_signal(barrier, 1, device_id=neighbour(n), device_id_type=mesh_id)
    for step in range(1, members):
        pl.semaphore_signal(barrier, 1, device_id={"blk": member(step)}, device_id_type=mesh_id)

    def widen(f, carry):
        wide[pl.ds(f * deep, height), :] = flux[f].astype(jnp.float32)
        return carry

    loads[0].wait()
    lax.fori_loop(0, fields, widen, 0, unroll=8)
    for side, first in enumerate((height - 2, 0)):
        for r in range(2):
            row = wide[pl.ds(first + r, fields, stride=deep), :]
            row_out[side, r] = row.astype(jnp.bfloat16)

    line = lax.broadcasted_iota(jnp.int32, (16, breadth), 0)
    column = lax.broadcasted_iota(jnp.int32, (16, breadth), 1)
    wanted = jnp.where(line < 2, breadth - 2 + line, line - 2)
    chosen = jnp.where((column == wanted) & (line < 4), 1.0, 0.0).astype(jnp.bfloat16)
    fill = jnp.zeros((LANES - fields, breadth), jnp.float32)

    def pick(i, carry):
        block = jnp.concatenate([wide[pl.ds(i, fields, stride=deep), :], fill], axis=0)
        picked = lax.dot_general(
            chosen,
            block.astype(jnp.bfloat16),
            (((1,), (1,)), ((), ())),
            preferred_element_type=jnp.float32,
        )
        edges[pl.ds(pl.multiple_of(i * 8, 8), 8), :] = picked[:8]
        return carry

    lax.fori_loop(0, height, pick, 0, unroll=8)
    for side in range(2):
        for q in range(2):
            col = edges[pl.ds(2 * side + q, height, stride=8), :]
            col_out[side, q] = col.astype(jnp.bfloat16)

    pl.semaphore_wait(barrier, members + 1)
    halos = []
    for n in range(4):
        source, target = (row_out, row_in) if n < 2 else (col_out, col_in)
        halos.append(
            pltpu.make_async_remote_copy(
                src_ref=source.at[n % 2],
                dst_ref=target.at[n % 2],
                send_sem=halo_sent.at[n],
                recv_sem=halo_came.at[n],
                device_id=neighbour(n),
                device_id_type=mesh_id,
            )
        )
        halos[-1].start()

    total[...] = jnp.zeros_like(total)
    gap = jnp.zeros((LEFT, LANES), jnp.float32)
    grid[(height + 4) * pitch :, :] = jnp.zeros((4 * pitch, LANES), jnp.float32)

    def place(row, block):
        start = row * pitch
        turned = jnp.concatenate([block, fill], axis=0).T
        grid[pl.ds(start, LEFT), :] = gap
        grid[pl.ds(start + LEFT, breadth), :] = turned
        grid[pl.ds(start + LEFT + breadth, LEFT), :] = gap

    def turn(i, carry):
        place(i + 2, wide[pl.ds(i, fields, stride=deep), :])
        return carry

    lax.fori_loop(0, height, turn, 0, unroll=4)

    for load in loads[1:]:
        load.wait()
    cell = cells[...]
    bases[...] = cell + lax.shift_right_logical(cell, shift) * (pitch - breadth)
    placing = pltpu.make_async_copy(bases, places, placed)
    placing.start()
    w = weight[...]
    ox = offset[0]
    oy = offset[1]
    moments = [
        jnp.sum(w, axis=0),
        jnp.sum(w * ox, axis=0) / 12.0,
        jnp.sum(w * oy, axis=0) / 12.0,
        0.5 * jnp.sum(w * ox * ox, axis=0) / 12.0,
        0.5 * jnp.sum(w * oy * oy, axis=0) / 12.0,
    ]
    mom[...] = jnp.zeros_like(mom)
    slots = lax.broadcasted_iota(jnp.int32, (1, capacity), 1)
    alive = [slots < count[k] for k in range(members)]
    for m, moment in enumerate(moments):
        for part in range(PARTS):
            piece = moment.astype(jnp.bfloat16).astype(jnp.float32)
            moment = moment - piece
            for k in range(members):
                mom[k, part * 8 + m : part * 8 + m + 1, :] = jnp.where(
                    alive[k], piece[k : k + 1, :], 0.0
                )

    placing.wait()
    for halo in halos:
        halo.wait()
    panel = lax.axis_index("panel")
    has_above = jnp.where(panel > 0, 1.0, 0.0)
    has_below = jnp.where(panel < lax.axis_size("panel") - 1, 1.0, 0.0)
    for r in range(2):
        place(r, row_in[0, r].astype(jnp.float32) * has_above)
        place(height + 2 + r, row_in[1, r].astype(jnp.float32) * has_below)
    for q in range(2):
        grid[pl.ds(2 * pitch + LEFT - 2 + q, height, stride=pitch), :] = col_in[0, q].astype(
            jnp.float32
        )
        grid[pl.ds(2 * pitch + LEFT + breadth + q, height, stride=pitch), :] = col_in[1, q].astype(
            jnp.float32
        )

    slot_group = lax.broadcasted_iota(jnp.int32, (LANES, GROUP * TAPS), 0) % GROUP
    tap_group = lax.broadcasted_iota(jnp.int32, (LANES, GROUP * TAPS), 1) // TAPS
    diagonal = slot_group == tap_group

    def gather(k, step, start):
        m = mom[k, :, pl.ds(start, LANES)].T.astype(jnp.bfloat16)
        coef = jnp.dot(m, pattern[...], preferred_element_type=jnp.float32)
        coef = jnp.where(diagonal, coef, 0.0)
        high = coef.astype(jnp.bfloat16)
        low = (coef - high.astype(jnp.float32)).astype(jnp.bfloat16)
        parts = []
        for g in range(LANES // GROUP):
            taps = []
            for s in range(GROUP):
                base = places[k, start + g * GROUP + s]
                taps.append(grid[pl.ds(base + 2 * pitch + LEFT - 2, 8), :])
                taps.append(grid[pl.ds(base + LEFT, 8, stride=pitch), :])
            picked = jnp.concatenate(taps, axis=0).astype(jnp.bfloat16)
            some = slice(g * GROUP, (g + 1) * GROUP)
            both = jnp.concatenate([high[some], low[some]], axis=0)
            r = jnp.dot(both, picked, preferred_element_type=jnp.float32)
            parts.append(r[:GROUP] + r[GROUP:])
        record = jnp.concatenate(parts, axis=0).T
        records[step - 1, :, pl.ds(start, LANES)] = record[:fields].astype(jnp.bfloat16)

    def send(step):
        return pltpu.make_async_remote_copy(
            src_ref=records.at[step - 1],
            dst_ref=landed.at[step - 1],
            send_sem=sent.at[step - 1],
            recv_sem=came.at[step - 1],
            device_id={"blk": member(step)},
            device_id_type=mesh_id,
        )

    rest = jnp.zeros((rows - fields, capacity), jnp.bfloat16)

    def deposit(record, source):
        cell = targets[pl.ds(source, 1), :]
        high = lax.shift_right_logical(cell, LOW.bit_length() - 1)
        low = cell & (LOW - 1)
        spots = lax.broadcasted_iota(jnp.int32, (LOW, capacity), 0)
        table = jnp.where(spots == low, 1.0, 0.0).astype(jnp.bfloat16)
        record = jnp.concatenate([record, rest], axis=0)
        for h in range(digits):
            here = jnp.where(high == h, 1.0, 0.0).astype(jnp.bfloat16)
            masked[h * rows : (h + 1) * rows, :] = record * here
        total[...] += lax.dot_general(
            masked[...], table, (((1,), (1,)), ((), ())), preferred_element_type=jnp.float32
        )

    def arrival(step, carry):
        send(step).wait_recv()
        deposit(landed[step - 1], lax.rem(me - step + members, members))
        return carry

    def advance(step, carry):
        def pair(p, inner):
            for c in range(PAIR):
                gather(member(step), step, pl.multiple_of((p * PAIR + c) * LANES, LANES))
            return inner

        lax.fori_loop(0, chunks // PAIR, pair, 0)

        @pl.when(step < members)
        def _():
            send(step).start()

        @pl.when(step > LAG)
        def _():
            arrival(step - LAG, 0)

        return carry

    lax.fori_loop(1, members + 1, advance, 0)
    deposit(records[members - 1], me)
    lax.fori_loop(members + 1 - LAG, members, arrival, 0)
    for h in range(digits):
        columns = slice(h * LOW, (h + 1) * LOW)
        out[:, columns] = total[h * rows : h * rows + fields, :]

    def finish(step, carry):
        send(step).wait_send()
        return carry

    lax.fori_loop(1, members, finish, 0)


def on_device(
    source_flux, gauss_weight, gauss_offset, slot_count, source_cell, target_cell, target_area
):
    fields, height, breadth = source_flux.shape
    members, capacity = source_cell.shape
    ocean_cells = target_area.shape[0]
    pitch = breadth + 2 * LEFT + 1
    digits = ocean_cells // LOW
    rows = -(-fields // 16) * 16
    vmem = pl.BlockSpec(memory_space=pltpu.VMEM)
    smem = pl.BlockSpec(memory_space=pltpu.SMEM)
    hbm = pl.BlockSpec(memory_space=pltpu.HBM)
    pattern = jnp.asarray(tap_pattern(), jnp.bfloat16)
    integrated = pl.pallas_call(
        remap_kernel,
        out_shape=jax.ShapeDtypeStruct((fields, ocean_cells), jnp.float32),
        in_specs=[smem] + [hbm] * 6,
        out_specs=vmem,
        scratch_shapes=[
            pltpu.VMEM(source_cell.shape, jnp.int32),
            pltpu.VMEM(source_cell.shape, jnp.int32),
            pltpu.SMEM(source_cell.shape, jnp.int32),
            pltpu.VMEM(source_flux.shape, jnp.bfloat16),
            pltpu.VMEM(gauss_weight.shape, jnp.float32),
            pltpu.VMEM(gauss_offset.shape, jnp.float32),
            pltpu.VMEM(pattern.shape, jnp.bfloat16),
            pltpu.VMEM(target_cell.shape, jnp.int32),
            pltpu.SemaphoreType.DMA((6,)),
            pltpu.SemaphoreType.DMA,
            pltpu.VMEM((fields * (height + 1), breadth), jnp.float32),
            pltpu.VMEM(((height + 8) * pitch, LANES), jnp.float32),
            pltpu.VMEM((height * 8, LANES), jnp.float32),
            pltpu.VMEM((members, 8 * PARTS, capacity), jnp.float32),
            pltpu.VMEM((2, 2, fields, breadth), jnp.bfloat16),
            pltpu.VMEM((2, 2, height, LANES), jnp.bfloat16),
            pltpu.VMEM((2, 2, fields, breadth), jnp.bfloat16),
            pltpu.VMEM((2, 2, height, LANES), jnp.bfloat16),
            pltpu.VMEM((members, fields, capacity), jnp.bfloat16),
            pltpu.VMEM((members - 1, fields, capacity), jnp.bfloat16),
            pltpu.VMEM((digits * rows, capacity), jnp.bfloat16),
            pltpu.VMEM((digits * rows, LOW), jnp.float32),
            pltpu.SemaphoreType.DMA((4,)),
            pltpu.SemaphoreType.DMA((4,)),
            pltpu.SemaphoreType.DMA((members - 1,)),
            pltpu.SemaphoreType.DMA((members - 1,)),
        ],
        compiler_params=pltpu.CompilerParams(
            vmem_limit_bytes=63 * 2**20, collective_id=0, has_side_effects=True
        ),
        name="remap",
    )(
        slot_count,
        source_cell,
        source_flux,
        gauss_weight,
        gauss_offset,
        pattern,
        target_cell,
    )
    return (integrated / target_area[None, :]).astype(jnp.bfloat16)


def solution(mesh):
    placed = (
        P(None, "panel", "blk"),
        P(None, ("panel", "blk"), None),
        P(None, None, ("panel", "blk"), None),
        P(("panel", "blk")),
        P(("panel", "blk"), None),
        P(("panel", "blk"), None),
        P(("panel", "blk")),
    )
    return jax.shard_map(
        on_device, mesh=mesh, in_specs=placed, out_specs=P(None, ("panel", "blk")), check_vma=False
    )
```
